32 devices in a mesh: sec: 4 (over x, core), space: 8 (over z, y).
Axes of the slice: x: 2, y: 2, z: 4, core: 2. Of those that a mesh axis runs over, the one named last changes fastest.
Arguments:
- droplet_integrals: float32 [64, 5, 64, 2048], P('sec', None, 'space'), may hold values from -3 to 3, as said below
- flow_number_lengthwise: float32 [64], P('sec'), may hold values from -0.6 to 0.6
- flow_number_crosswise: float32 [64], P('sec'), may hold values from -0.35 to 0.35
- inflow_boundary_integrals: float32 [64, 5], P('sec'), may hold values from 0.2 to 2
- boundary_wall_indicator: int32 [64, 2048], P('space'), may hold values 0 or 1
- inflow_indicator: int32 [64, 2048], P('space'), may hold values 0 or 1
- collision_coefficient: float32 [64, 64], replicated, may hold values from 0.0005 to 0.008
- collision_target_share: float32 [64, 64], replicated, may hold values from 0 to 0.03
- evaporation_speed_stepwise: float32 [64], replicated, may hold values from 0.01 to 0.1
- thermal_factor: float32 [64, 2048], P('space', 'sec'), may hold values from 0.5 to 2
Outputs:
- spray: float32 [64, 5, 64, 2048], P(None, None, 'space', 'sec')
- gas_source: float32 [5, 64, 2048], P(None, 'space', 'sec')
The draws below stay inside these ranges and needn't reach their ends.
Inputs may be any that keep to these rules, and one draw needn't show every extreme that they name: `droplet_integrals`: moment 0 (mass) is positive, 0.1 or more, in every section and cell.
All inputs are finite; a program needn't handle non-finite values. No bound on the sum of `boundary_wall_indicator` or of `inflow_indicator` on one device may be relied on, other than what follows from the above.
Results may differ from the reference program's by a relative error of at most 0.000084.
Values sent between devices are 32-bit elements; how exact they have to be, the bound alone decides.
No kernel may reach another device: no remote copies, remote signals or barrier semaphores. Data moves between devices by JAX's collectives and lax.ppermute only.
A program may use at most 128 MiB of HBM per device.

```python
import math
import jax
import jax.numpy as jnp
from jax import lax

SECTIONS = 64
MOM = 5
SUB = 4
GRID_COLUMN_SPAN = 2048
GRID_ROWS_COUNT = 64


def draw_droplet_integrals(key, part):
    mass_key, rest_key = jax.random.split(jax.random.fold_in(key, 11))
    mass_part = jnp.exp(jax.random.uniform(mass_key, (SECTIONS, 1, GRID_ROWS_COUNT, GRID_COLUMN_SPAN), jnp.float32, math.log(0.2), math.log(2.0)))
    rest_part = jnp.clip(0.5 * jax.random.normal(rest_key, (SECTIONS, MOM - 1, GRID_ROWS_COUNT, GRID_COLUMN_SPAN), jnp.float32), -3.0, 3.0)
    return jnp.concatenate([mass_part, rest_part], axis=1)


def plant(array, rng, least, largest):
    spot = [jax.random.randint(jax.random.fold_in(rng, axis), (), 0, length) for axis, length in enumerate(array.shape)]
    widest = array.shape.index(max(array.shape))
    neighbour = spot[:widest] + [(spot[widest] + 1) % array.shape[widest]] + spot[widest + 1:]
    return array.at[tuple(spot)].set(least).at[tuple(neighbour)].set(largest)


def shard_levels(rng, extent, pieces, smallest, largest):
    gain, own = 1.0, jax.random.fold_in(rng, 6)
    for position, blocks in pieces:
        steps = jnp.exp(jax.random.uniform(jax.random.fold_in(own, position), (blocks,), jnp.float32, smallest / len(pieces), largest / len(pieces)))
        gain = gain * jnp.repeat(steps, extent[position] // blocks).reshape([-1 if axis == position else 1 for axis in range(len(extent))])
    return gain


def setup_inputs(seed: int = 0) -> dict:
    splits = jax.random.split(jax.random.key(seed), 11)
    droplet_integrals = draw_droplet_integrals(jax.random.fold_in(splits[10], 71), 0)
    flow_number_lengthwise = jnp.clip(jax.random.uniform(splits[1], (SECTIONS,), jnp.float32, -0.6, 0.6) * shard_levels(splits[1], (SECTIONS,), ((0, 4),), -0.4, 0.0), -0.6, 0.6)
    flow_number_crosswise = jnp.clip(jax.random.uniform(splits[2], (SECTIONS,), jnp.float32, -0.35, 0.35) * shard_levels(splits[2], (SECTIONS,), ((0, 4),), -0.4, 0.0), -0.35, 0.35)
    inflow_boundary_integrals = jnp.clip(0.2 + 1.8 * jax.random.uniform(splits[3], (SECTIONS, MOM), jnp.float32) ** shard_levels(splits[3], (SECTIONS, MOM), ((0, 4),), -0.2, 0.2), 0.2, 2.0)
    boundary_wall_indicator = plant((jax.random.randint(splits[4], (GRID_ROWS_COUNT, GRID_COLUMN_SPAN), 0, 16) < 1).astype(jnp.int32), jax.random.fold_in(splits[4], 1), 0, 1)
    inflow_indicator = plant((jax.random.randint(splits[5], (GRID_ROWS_COUNT, GRID_COLUMN_SPAN), 0, 32) < 1).astype(jnp.int32), jax.random.fold_in(splits[5], 1), 0, 1)
    collision_coefficient = jnp.clip(jnp.exp(jax.random.uniform(splits[6], (SECTIONS, SECTIONS), jnp.float32, math.log(0.0005), math.log(0.008))), 0.0005, 0.008)
    collision_target_share = jnp.clip(jax.random.uniform(splits[7], (SECTIONS, SECTIONS), jnp.float32, 0.0, 0.03), 0.0, 0.03)
    evaporation_speed_stepwise = jnp.clip(jnp.exp(jax.random.uniform(splits[8], (SECTIONS,), jnp.float32, math.log(0.01), math.log(0.1))), 0.01, 0.1)
    thermal_factor = jnp.clip(jnp.exp(math.log(2.0) - 1.3862944 * jax.random.uniform(splits[9], (GRID_ROWS_COUNT, GRID_COLUMN_SPAN), jnp.float32) ** shard_levels(splits[9], (GRID_ROWS_COUNT, GRID_COLUMN_SPAN), ((0, 8), (1, 4)), -0.2, 0.2)), 0.5, 2.0)
    return dict(droplet_integrals=droplet_integrals, flow_number_lengthwise=flow_number_lengthwise, flow_number_crosswise=flow_number_crosswise, inflow_boundary_integrals=inflow_boundary_integrals, boundary_wall_indicator=boundary_wall_indicator, inflow_indicator=inflow_indicator, collision_coefficient=collision_coefficient, collision_target_share=collision_target_share, evaporation_speed_stepwise=evaporation_speed_stepwise, thermal_factor=thermal_factor)


def advance(padded, speed_x, speed_y, inflow_value, inflow_rows, wall_rows):
    middle = padded[..., 1:-1, :]
    western = padded[..., :-2, :]
    eastern = padded[..., 2:, :]
    border = jnp.zeros_like(middle[..., :1])
    southern = jnp.concatenate([border, middle[..., :-1]], axis=-1)
    northern = jnp.concatenate([middle[..., 1:], border], axis=-1)
    transported_integrals = middle - jnp.maximum(speed_x, 0.0) * (middle - western) - jnp.minimum(speed_x, 0.0) * (eastern - middle)
    transported_integrals = transported_integrals - jnp.maximum(speed_y, 0.0) * (middle - southern) - jnp.minimum(speed_y, 0.0) * (northern - middle)
    transported_integrals = jnp.where(inflow_rows > 0, inflow_value, transported_integrals)
    return jnp.where(wall_rows > 0, jnp.zeros_like(transported_integrals), transported_integrals)


def couple(cell_block, collision_coefficient, collision_target_share):
    mass_part = cell_block[:, 0]
    merge_rate = jnp.einsum("sj,jxy->sxy", collision_coefficient, mass_part, precision=lax.Precision.HIGHEST)
    flux_terms = cell_block * merge_rate[:, None]
    gained = jnp.einsum("sj,jmxy->smxy", collision_target_share, flux_terms, precision=lax.Precision.HIGHEST)
    return cell_block - flux_terms + gained


def reference(droplet_integrals, flow_number_lengthwise, flow_number_crosswise, inflow_boundary_integrals, boundary_wall_indicator, inflow_indicator, collision_coefficient, collision_target_share, evaporation_speed_stepwise, thermal_factor):
    def move_one(items):
        field, speed_x, speed_y, inflow_row = items
        for substep in range(SUB):
            padded = jnp.pad(field, ((0, 0), (1, 1), (0, 0)))
            field = advance(padded, speed_x, speed_y, inflow_row[:, None, None], inflow_indicator, boundary_wall_indicator)
        return field

    transported_integrals = lax.map(move_one, (droplet_integrals, flow_number_lengthwise, flow_number_crosswise, inflow_boundary_integrals))
    evaporated_quantity = evaporation_speed_stepwise[:, None, None, None] * thermal_factor[None, None] * transported_integrals
    gas_source = jnp.sum(evaporated_quantity, axis=0)
    remaining = transported_integrals - evaporated_quantity
    spray = couple(remaining, collision_coefficient, collision_target_share)
    return spray, gas_source
```

```python
import functools

import jax
import jax.numpy as jnp
from jax import lax
from jax.experimental import pallas as pl
from jax.experimental.pallas import tpu as pltpu
from jax.sharding import PartitionSpec as P

SUB = 4
ROWS = 2 * SUB
LANES = 128
TILE = 8
F32 = jnp.float32
BF16 = jnp.bfloat16
PLAN = ((0, "y"), (1, "y"), (2, "z"), (3, "z"), (4, "z"))
SELECT = ((0, 2), (1, 3, 4))
TOGETHER_INNER = 5
TOGETHER_OUTER = 4
VMEM_LIMIT = 48 * 1024 * 1024


def stacked(array):
    *lead, rows, columns = array.shape
    tiles = columns // LANES
    array = array.reshape(*lead, rows, tiles, LANES)
    return jnp.swapaxes(array, -3, -2).reshape(*lead, rows * tiles, LANES)


def sublane(shape=(TILE, LANES)):
    return lax.broadcasted_iota(jnp.int32, shape, 0)


class Wind:
    def __init__(self, speed_x, speed_y, blocks):
        self.a, self.b = jnp.abs(speed_x), jnp.abs(speed_y)
        self.own = 1.0 - self.a - self.b
        self.blocks = blocks
        self.positive_x = speed_x > 0.0
        self.positive_y = speed_y > 0.0
        lane = lax.broadcasted_iota(jnp.int32, (TILE, LANES), 1)
        self.lane_shift = jnp.where(self.positive_y, 1, LANES - 1).astype(jnp.int32)
        self.band_shift = jnp.where(self.positive_y, 1, TILE - 1).astype(jnp.int32)
        self.edge = lane == jnp.where(self.positive_y, 0, LANES - 1)
        self.border = sublane() == jnp.where(self.positive_y, 0, TILE - 1)

    def row(self, u, first, last):
        return jnp.where(self.positive_x, first + u, last - u)

    def block(self, j):
        return jnp.where(self.positive_y, j, self.blocks - 1 - j)


def substeps(chains):
    states = [chain[1] for chain in chains]
    for step in range(1, SUB + 1):
        fresh = []
        for (wind, _, code, value), state in zip(chains, states):
            rows = [None] * step
            for u in range(step, ROWS):
                turned = [pltpu.roll(tile, wind.lane_shift, axis=1) for tile in state[u]]
                wrap = pltpu.roll(turned[-1], wind.band_shift, axis=0)
                behind = [jnp.where(wind.border, 0.0, wrap)] + turned[:-1]
                tiles = []
                for j, tile in enumerate(state[u]):
                    side = jnp.where(wind.edge, behind[j], turned[j])
                    moved = wind.own * tile + wind.a * state[u - 1][j] + wind.b * side
                    kind = code(u, j)
                    tiles.append(jnp.where(kind < 0.0, moved, kind * value))
                rows.append(tiles)
            fresh.append(rows)
        states = fresh
    return states


def keep(wind, state, packed):
    blocks = wind.blocks
    for u in range(SUB, ROWS):
        row = wind.row(u, -SUB, ROWS - 1)
        for j, tile in enumerate(state[u]):
            packed[pl.ds(row * blocks + wind.block(j), TILE, stride=SUB * blocks), :] = tile


def scatter(packed, me, outs):
    share = packed.shape[0] // len(outs)
    for k, (out, spot) in enumerate(outs):
        start = pl.multiple_of((me ^ k) * share, share)
        out[spot] = packed[pl.ds(start, share), :]


def select_kernel(coded, count, blocks, ux_ref, *refs):
    if coded:
        (wall_ref, inflow_ref), refs = refs[:2], refs[2:]
    x_refs, out_refs = refs[:count], refs[count : 2 * count]
    per_step = x_refs[0].shape[0]
    step = pl.program_id(0)
    spacing = blocks * ROWS

    def section(s, carry):
        first = jnp.where(ux_ref[step * per_step + s] > 0.0, SUB, 0)
        for x_ref, out_ref in zip(x_refs, out_refs):
            for row in range(SUB):
                for block in range(blocks):
                    spot = (row * blocks + block) * TILE
                    out_ref[s, spot : spot + TILE, :] = x_ref[
                        s, pl.ds(block * ROWS + first + row, TILE, stride=spacing), :
                    ]
        return carry

    lax.fori_loop(0, per_step, section, 0, unroll=2)
    if coded:
        code_ref = refs[-1]

        @pl.when(step == 0)
        def _():
            for row in range(ROWS):
                for block in range(blocks):
                    spot = (row * blocks + block) * TILE
                    source = pl.ds(block * ROWS + row, TILE, stride=spacing)
                    inflow = jnp.where(inflow_ref[source, :] > 0, 1.0, -1.0)
                    code_ref[spot : spot + TILE, :] = jnp.where(
                        wall_ref[source, :] > 0, 0.0, inflow
                    )


def inner_kernel(moments, blocks, together, me_ref, ux_ref, uy_ref, inflow_ref, code_ref, x_ref, *rest):
    *out_refs, packed = rest
    per_step = x_ref.shape[0]
    step = pl.program_id(0)
    me = me_ref[0]
    spacing = blocks * ROWS
    size = x_ref.shape[1] // moments
    share = out_refs[0].shape[1] // moments

    def section(s, carry):
        number = step * per_step + s
        wind = Wind(ux_ref[number], uy_ref[number], blocks)

        def code(u, j):
            spot = (wind.row(u, 0, ROWS - 1) * blocks + wind.block(j)) * TILE
            return code_ref[pl.ds(pl.multiple_of(spot, TILE), TILE), :]

        for low in range(0, moments, together):
            some = range(low, min(moments, low + together))
            chains = []
            for m in some:
                tiles = [
                    [
                        x_ref[
                            s,
                            pl.ds(
                                m * size + wind.block(j) * ROWS + wind.row(u, 0, ROWS - 1),
                                TILE,
                                stride=spacing,
                            ),
                            :,
                        ]
                        for j in range(blocks)
                    ]
                    for u in range(ROWS)
                ]
                chains.append((wind, tiles, code, inflow_ref[number, m]))
            for m, state in zip(some, substeps(chains)):
                keep(wind, state, packed.at[m])
        for m in range(moments):
            scatter(
                packed.at[m],
                me,
                [(out, (s, slice(m * share, (m + 1) * share))) for out in out_refs],
            )
        return carry

    lax.fori_loop(0, per_step, section, 0)


def outer_kernel(
    moment, halos, blocks, together, me_ref, odd_ref, ux_ref, uy_ref, inflow_ref,
    before_ref, after_ref, code_ref, x_ref, *rest
):
    halo_refs, out_refs, (codes, packed) = rest[:halos], rest[halos:-2], rest[-2:]
    per_step = x_ref.shape[0]
    step = pl.program_id(0)
    me = me_ref[0]
    odd = odd_ref[0]
    spacing = blocks * ROWS
    edge = SUB * blocks * TILE
    codes[:edge] = before_ref[...]
    codes[edge : 2 * edge] = after_ref[...]
    codes[2 * edge :] = code_ref[...]

    def sections(turn, carry):
        chains = []
        for i in range(together):
            s = turn * together + i
            number = step * per_step + s
            wind = Wind(ux_ref[number], uy_ref[number], blocks)
            outside = jnp.where(wind.positive_x, 0, edge)
            second = jnp.logical_xor(wind.positive_x, odd == 1)

            def code(u, j, wind=wind, outside=outside):
                if u < SUB:
                    spot = outside + (wind.row(u, 0, SUB - 1) * blocks + wind.block(j)) * TILE
                else:
                    row = wind.row(u, -SUB, ROWS + SUB - 1)
                    spot = 2 * edge + (row * blocks + wind.block(j)) * TILE
                return codes[pl.ds(pl.multiple_of(spot, TILE), TILE), :]

            tiles = []
            for u in range(ROWS):
                row = []
                for j in range(blocks):
                    if u < SUB:
                        spot = (wind.row(u, 0, SUB - 1) * blocks + wind.block(j)) * TILE
                        spot = pl.ds(pl.multiple_of(spot, TILE), TILE)
                        tile = halo_refs[0][s, spot, :]
                        if halos == 2:
                            tile = jnp.where(second, halo_refs[1][s, spot, :], tile)
                    else:
                        start = wind.block(j) * ROWS + wind.row(u, -SUB, ROWS + SUB - 1)
                        tile = x_ref[s, pl.ds(start, TILE, stride=spacing), :]
                    row.append(tile)
                tiles.append(row)
            chains.append((wind, tiles, code, inflow_ref[number, moment]))
        for i, (chain, state) in enumerate(zip(chains, substeps(chains))):
            keep(chain[0], state, packed.at[i])
        for i in range(together):
            number = step * per_step + turn * together + i
            scatter(packed.at[i], me, [(out, number) for out in out_refs])
        return carry

    lax.fori_loop(0, per_step // together, sections, 0)
    if moment == 0:

        @pl.when(step == 0)
        def _():
            size = out_refs[0].shape[1]
            for number in range(size):
                line = jnp.full((1, LANES), ux_ref[number], F32)
                for out in out_refs:
                    out[size, number : number + 1, :] = line


def split_dot(weights, values):
    high = values.astype(BF16)
    rest = (values - high.astype(F32)).astype(BF16)
    return jnp.dot(
        weights, jnp.concatenate([high, rest, high], axis=0), preferred_element_type=F32
    )


def couple_kernel(first, groups, group_size, blocks, *refs):
    me_ref, rate_ref, share_ref, thermal_ref = refs[:4]
    refs = refs[4:]
    sign_refs, inner, outer = refs[:groups], refs[groups : 2 * groups], refs[2 * groups : 3 * groups]
    refs = refs[3 * groups :]
    if first:
        kernel_ref, spray_ref, gas_ref, merge_ref, *scratch = refs
    else:
        merge_ref, _, _, spray_ref, gas_ref, *scratch = refs
    rest, made, total = scratch
    me = me_ref[0]
    sections = groups * group_size
    size = ROWS * blocks
    half = size // 2
    thermal = [thermal_ref[:half, :], thermal_ref[half:, :]]
    gas = tuple(jnp.zeros((half, LANES), F32) for _ in thermal)
    for k in range(groups):

        def section(s, sums, k=k):
            number = (me ^ k) * group_size + s
            flip = jnp.broadcast_to(sign_refs[k][0, pl.ds(s, 1), :], (half, LANES)) > 0.0
            rate = rate_ref[number]
            one, two = inner[k][s], outer[k][s]
            result = []
            for i, moved in enumerate((jnp.where(flip, two, one), jnp.where(flip, one, two))):
                evaporated = (rate * thermal[i]) * moved
                result.append(sums[i] + evaporated)
                rest[pl.ds(pl.multiple_of(number * size + i * half, half), half), :] = moved - evaporated
            return tuple(result)

        gas = lax.fori_loop(0, group_size, section, gas, unroll=4)
    for i in range(2):
        total[i * half : (i + 1) * half, :] = gas[i]
    for block in range(blocks):
        gas_ref[0, :, block * LANES : (block + 1) * LANES] = total[pl.ds(block, ROWS, stride=blocks), :]
    for row in range(ROWS):
        spots = [pl.ds(row * blocks + block, sections, stride=size) for block in range(blocks)]
        cells = jnp.concatenate([rest[spot, :] for spot in spots], axis=1)
        if first:
            merge = split_dot(kernel_ref[...], cells)
            merge_ref[row] = merge
        else:
            merge = merge_ref[row]
        flux = cells * merge
        result = cells - flux + split_dot(share_ref[...], flux)
        for block, spot in enumerate(spots):
            made[spot, :] = result[:, block * LANES : (block + 1) * LANES]

    def write(s, carry):
        for block in range(blocks):
            spray_ref[s, 0, :, block * LANES : (block + 1) * LANES] = made[
                pl.ds(s * size + block, ROWS, stride=blocks), :
            ]
        return carry

    lax.fori_loop(0, sections, write, 0, unroll=8)


def params(**more):
    return pltpu.CompilerParams(vmem_limit_bytes=VMEM_LIMIT, **more)


def split_weights(weights):
    high = lax.reduce_precision(weights, 8, 7)
    return jnp.concatenate([high, high, weights - high], axis=1).astype(BF16)


def shards(
    droplet_integrals,
    flow_number_lengthwise,
    flow_number_crosswise,
    inflow_boundary_integrals,
    boundary_wall_indicator,
    inflow_indicator,
    collision_coefficient,
    collision_target_share,
    evaporation_speed_stepwise,
    thermal_factor,
):
    x, ux, uy = droplet_integrals, flow_number_lengthwise, flow_number_crosswise
    group_size, moments, rows, columns = x.shape
    groups = lax.axis_size("sec")
    slabs = lax.axis_size("space")
    sections = groups * group_size
    width = columns // groups
    blocks = columns // (TILE * LANES)
    size = columns // LANES * ROWS
    share_size = size // 2 // groups
    assert rows == ROWS and slabs % 2 == 0 and TILE % groups == 0

    me = lax.axis_index("sec").astype(jnp.int32).reshape(1)
    odd = (lax.axis_index("space") % 2).astype(jnp.int32).reshape(1)

    swap = [(i, i ^ 1) for i in range(slabs)]
    outward = [(i, i + 2) for i in range(0, slabs - 2, 2)] + [(i, i - 2) for i in range(3, slabs, 2)]
    inward = [(j, i) for i, j in outward]

    smem = pl.BlockSpec(memory_space=pltpu.SMEM)
    anywhere = pl.BlockSpec(memory_space=pl.ANY)
    cells = stacked(x).reshape(group_size, moments * size, LANES)

    def moment_spec(per_step, moment):
        return pl.BlockSpec((per_step, size, LANES), lambda g: (g, moment, 0))

    chosen = {}
    code = None
    edge = SUB * blocks * TILE
    for some in SELECT:
        coded = code is None
        per_step = group_size // 2
        in_specs, operands = [smem], [ux]
        out_specs = [pl.BlockSpec((per_step, edge, LANES), lambda g: (g, 0, 0))] * len(some)
        out_shape = [jax.ShapeDtypeStruct((group_size, edge, LANES), F32)] * len(some)
        if coded:
            flat = pl.BlockSpec((size, LANES), lambda g: (0, 0))
            in_specs += [flat] * 2
            operands += [stacked(boundary_wall_indicator), stacked(inflow_indicator)]
            out_specs.append(flat)
            out_shape.append(jax.ShapeDtypeStruct((size, LANES), F32))
        made = pl.pallas_call(
            functools.partial(select_kernel, coded, len(some), blocks),
            grid=(group_size // per_step,),
            in_specs=in_specs + [moment_spec(per_step, moment) for moment in some],
            out_specs=out_specs,
            out_shape=out_shape,
            compiler_params=params(),
            cost_estimate=pl.CostEstimate(
                flops=x.size, bytes_accessed=x.size * 6 * len(some) // moments, transcendentals=0
            ),
            name="select_upwind_rows",
        )(*operands, *[cells] * len(some))
        if coded:
            code = made[-1]
        chosen.update(zip(some, made))

    before = lax.ppermute(code[edge:], "space", [(i, i + 1) for i in range(slabs - 1)])
    after = lax.ppermute(code[:edge], "space", [(i + 1, i) for i in range(slabs - 1)])

    per_step = 2
    inner = pl.pallas_call(
        functools.partial(inner_kernel, moments, blocks, TOGETHER_INNER),
        grid=(group_size // per_step,),
        in_specs=[smem] * 4
        + [
            pl.BlockSpec((size, LANES), lambda g: (0, 0)),
            pl.BlockSpec((per_step, moments * size, LANES), lambda g: (g, 0, 0)),
        ],
        out_specs=[pl.BlockSpec((per_step, moments * share_size, LANES), lambda g: (g, 0, 0))]
        * groups,
        out_shape=[jax.ShapeDtypeStruct((group_size, moments * share_size, LANES), F32)] * groups,
        scratch_shapes=[pltpu.VMEM((moments, size // 2, LANES), F32)],
        compiler_params=params(),
        cost_estimate=pl.CostEstimate(
            flops=x.size * 20, bytes_accessed=x.size * 6, transcendentals=0
        ),
        name="transport_inner_rows",
    )(me, ux, uy, inflow_boundary_integrals, code, cells)

    def exchange(parts):
        return [parts[0]] + [
            lax.ppermute(parts[k], "sec", [(i, i ^ k) for i in range(groups)])
            for k in range(1, groups)
        ]

    inner = exchange(inner)

    per_step = group_size // 2
    outer = {}
    for moment, way in PLAN:
        if way == "y":
            near = lax.ppermute(chosen[moment], "space", swap)
            halos = [near, lax.ppermute(near, "space", outward)]
        else:
            far = lax.ppermute(chosen[moment], "space", inward)
            stays = (ux > 0.0) == (odd[0] == 0)
            relayed = jnp.where(stays[:, None, None], chosen[moment], far)
            halos = [lax.ppermute(relayed, "space", swap)]
        length = group_size + (moment == 0)
        flat = pl.BlockSpec((edge, LANES), lambda g: (0, 0))
        parts = pl.pallas_call(
            functools.partial(outer_kernel, moment, len(halos), blocks, TOGETHER_OUTER),
            grid=(group_size // per_step,),
            in_specs=[smem] * 5
            + [flat] * 2
            + [pl.BlockSpec((size, LANES), lambda g: (0, 0)), moment_spec(per_step, moment)]
            + [pl.BlockSpec((per_step, edge, LANES), lambda g: (g, 0, 0))] * len(halos),
            out_specs=[pl.BlockSpec((length, share_size, LANES), lambda g: (0, 0, 0))] * groups,
            out_shape=[jax.ShapeDtypeStruct((length, share_size, LANES), F32)] * groups,
            scratch_shapes=[
                pltpu.VMEM((2 * edge + size, LANES), F32),
                pltpu.VMEM((TOGETHER_OUTER, size // 2, LANES), F32),
            ],
            compiler_params=params(),
            cost_estimate=pl.CostEstimate(
                flops=x.size * 4, bytes_accessed=x.size * 2, transcendentals=0
            ),
            name="transport_outer_rows",
        )(me, odd, ux, uy, inflow_boundary_integrals, before, after, code, cells, *halos)
        outer[moment] = exchange(parts)

    share = split_weights(collision_target_share)
    kernel = split_weights(collision_coefficient)
    step_width = blocks * LANES
    steps = width // step_width
    step_size = ROWS * blocks
    thermal = thermal_factor.reshape(ROWS, steps, blocks, LANES).swapaxes(0, 1)
    thermal = thermal.reshape(steps * step_size, LANES)
    spray_type = jax.ShapeDtypeStruct((sections, moments, rows, width), F32)
    gas_type = jax.ShapeDtypeStruct((moments, rows, width), F32)
    merge_type = jax.ShapeDtypeStruct((rows, sections, width), F32)
    merge_spec = pl.BlockSpec((rows, sections, step_width), lambda j: (0, 0, j))
    spray = gas = merge = None
    for moment in [0] + [moment for moment, _ in PLAN if moment]:
        first = moment == 0
        in_specs = (
            [smem] * 2
            + [
                pl.BlockSpec(share.shape, lambda j: (0, 0)),
                pl.BlockSpec((step_size, LANES), lambda j: (j, 0)),
            ]
            + [pl.BlockSpec((1, share_size, LANES), lambda j: (group_size, 0, 0))] * groups
            + [
                pl.BlockSpec(
                    (group_size, step_size // 2, LANES),
                    lambda j, moment=moment: (0, moment * steps + j, 0),
                )
            ]
            * groups
            + [pl.BlockSpec((group_size, step_size // 2, LANES), lambda j: (0, j, 0))] * groups
        )
        operands = [me, evaporation_speed_stepwise, share, thermal]
        operands += list(outer[0]) + list(inner) + list(outer[moment])
        out_specs = [
            pl.BlockSpec((sections, 1, rows, step_width), lambda j, moment=moment: (0, moment, 0, j)),
            pl.BlockSpec((1, rows, step_width), lambda j, moment=moment: (moment, 0, j)),
        ]
        out_shape = [spray_type, gas_type]
        aliases = {}
        if first:
            in_specs.append(pl.BlockSpec(kernel.shape, lambda j: (0, 0)))
            operands.append(kernel)
            out_specs.append(merge_spec)
            out_shape.append(merge_type)
        else:
            aliases = {len(operands) + 1: 0, len(operands) + 2: 1}
            in_specs += [merge_spec, anywhere, anywhere]
            operands += [merge, spray, gas]
        made = pl.pallas_call(
            functools.partial(couple_kernel, first, groups, group_size, blocks),
            grid=(steps,),
            in_specs=in_specs,
            out_specs=out_specs,
            out_shape=out_shape,
            input_output_aliases=aliases,
            scratch_shapes=[pltpu.VMEM((sections * step_size, LANES), F32)] * 2
            + [pltpu.VMEM((step_size, LANES), F32)],
            compiler_params=params(),
            cost_estimate=pl.CostEstimate(
                flops=sections * rows * width * sections * 2,
                bytes_accessed=sections * rows * width * 12,
                transcendentals=0,
            ),
            name="couple_sections",
        )(*operands)
        if first:
            spray, gas, merge = made
        else:
            spray, gas = made
    return spray, gas


def solution(mesh):
    return jax.shard_map(
        shards,
        mesh=mesh,
        in_specs=(
            P("sec", None, "space", None),
            P("sec"),
            P("sec"),
            P("sec", None),
            P("space", None),
            P("space", None),
            P(),
            P(),
            P(),
            P("space", "sec"),
        ),
        out_specs=(P(None, None, "space", "sec"), P(None, "space", "sec")),
        check_vma=False,
    )
```

```python
import functools

import jax
import jax.numpy as jnp
from jax import lax
from jax.experimental import pallas as pl
from jax.experimental.pallas import tpu as pltpu
from jax.sharding import PartitionSpec as P

SUB = 4
ROWS = 2 * SUB
LANES = 128
TILE = 8
F32 = jnp.float32
BF16 = jnp.bfloat16
TOGETHER_INNER = 5
TOGETHER_OUTER = 4
VMEM_LIMIT = 48 * 1024 * 1024


def stacked(array):
    *lead, rows, columns = array.shape
    tiles = columns // LANES
    array = array.reshape(*lead, rows, tiles, LANES)
    return jnp.swapaxes(array, -3, -2).reshape(*lead, rows * tiles, LANES)


def sublane(shape=(TILE, LANES)):
    return lax.broadcasted_iota(jnp.int32, shape, 0)


class Wind:
    def __init__(self, speed_x, speed_y, blocks):
        self.a, self.b = jnp.abs(speed_x), jnp.abs(speed_y)
        self.own = 1.0 - self.a - self.b
        self.blocks = blocks
        self.positive_x = speed_x > 0.0
        self.positive_y = speed_y > 0.0
        lane = lax.broadcasted_iota(jnp.int32, (TILE, LANES), 1)
        self.lane_shift = jnp.where(self.positive_y, 1, LANES - 1).astype(jnp.int32)
        self.band_shift = jnp.where(self.positive_y, 1, TILE - 1).astype(jnp.int32)
        self.edge = lane == jnp.where(self.positive_y, 0, LANES - 1)
        self.border = sublane() == jnp.where(self.positive_y, 0, TILE - 1)

    def row(self, u, first, last):
        return jnp.where(self.positive_x, first + u, last - u)

    def block(self, j):
        return jnp.where(self.positive_y, j, self.blocks - 1 - j)


def substeps(chains):
    states = [chain[1] for chain in chains]
    for step in range(1, SUB + 1):
        fresh = []
        for (wind, _, code, value), state in zip(chains, states):
            rows = [None] * step
            for u in range(step, ROWS):
                turned = [pltpu.roll(tile, wind.lane_shift, axis=1) for tile in state[u]]
                wrap = pltpu.roll(turned[-1], wind.band_shift, axis=0)
                behind = [jnp.where(wind.border, 0.0, wrap)] + turned[:-1]
                tiles = []
                for j, tile in enumerate(state[u]):
                    side = jnp.where(wind.edge, behind[j], turned[j])
                    moved = wind.own * tile + wind.a * state[u - 1][j] + wind.b * side
                    kind = code(u, j)
                    tiles.append(jnp.where(kind < 0.0, moved, kind * value))
                rows.append(tiles)
            fresh.append(rows)
        states = fresh
    return states


def keep(wind, state, packed):
    blocks = wind.blocks
    for u in range(SUB, ROWS):
        row = wind.row(u, -SUB, ROWS - 1)
        for j, tile in enumerate(state[u]):
            packed[pl.ds(row * blocks + wind.block(j), TILE, stride=SUB * blocks), :] = tile


def scatter(packed, me, outs):
    share = packed.shape[0] // len(outs)
    for k, (out, spot) in enumerate(outs):
        start = pl.multiple_of((me ^ k) * share, share)
        out[spot] = packed[pl.ds(start, share), :]


def select_kernel(outs, blocks, ux_ref, *refs):
    count = sum(outs)
    x_refs, refs = refs[:count], refs[count:]
    coded = len(refs) > len(outs) + 1
    if coded:
        wall_hbm, inflow_hbm, *refs, wall_ref, inflow_ref, sems = refs
        refs = [None] + refs
    out_refs = refs[1 : 1 + len(outs)]
    per_step = x_refs[0].shape[0]
    step = pl.program_id(0)
    spacing = blocks * ROWS
    edge = SUB * blocks * TILE

    def loads():
        return (
            pltpu.make_async_copy(wall_hbm, wall_ref, sems.at[0]),
            pltpu.make_async_copy(inflow_hbm, inflow_ref, sems.at[1]),
        )

    if coded:

        @pl.when(step == 0)
        def _():
            for load in loads():
                load.start()

    def section(s, carry):
        number = step * per_step + s
        first = jnp.where(ux_ref[number] > 0.0, SUB, 0)
        sources = iter(x_refs)
        for held, out_ref in zip(outs, out_refs):
            for i in range(held):
                x_ref = next(sources)
                for row in range(SUB):
                    for block in range(blocks):
                        spot = i * edge + (row * blocks + block) * TILE
                        out_ref[number, spot : spot + TILE, :] = x_ref[
                            s, pl.ds(block * ROWS + first + row, TILE, stride=spacing), :
                        ]
        return carry

    lax.fori_loop(0, per_step, section, 0, unroll=2)
    if coded:
        code_ref = refs[-1]

        @pl.when(step == pl.num_programs(0) - 1)
        def _():
            for load in loads():
                load.wait()
            last = out_refs[0].shape[0] - 2
            for row in range(ROWS):
                for block in range(blocks):
                    spot = (row * blocks + block) * TILE
                    source = pl.ds(block * ROWS + row, TILE, stride=spacing)
                    inflow = jnp.where(inflow_ref[source, :] > 0, 1.0, -1.0)
                    kind = jnp.where(wall_ref[source, :] > 0, 0.0, inflow)
                    code_ref[spot : spot + TILE, :] = kind
                    spot -= edge * (row // SUB)
                    out_refs[0][last + row // SUB, spot : spot + TILE, :] = kind


def relay_kernel(moments, odd_ref, ux_ref, _, own_ref, far_ref, *out_refs):
    odd = odd_ref[0]
    sections, size = own_ref.shape[0], own_ref.shape[1] // moments

    def section(s, carry):
        def copy(source):
            for i, out_ref in enumerate(out_refs):
                out_ref[s] = source[s, i * size : (i + 1) * size, :]

        stays = (ux_ref[s] > 0.0) != (odd == 1)
        pl.when(stays)(lambda: copy(own_ref))
        pl.when(jnp.logical_not(stays))(lambda: copy(far_ref))
        return carry

    lax.fori_loop(0, sections, section, 0)


def inner_kernel(
    base, moments, blocks, together, me_ref, ux_ref, uy_ref, inflow_ref, _, code_ref, *rest
):
    x_refs, out_refs, packed = rest[:moments], rest[moments:-1], rest[-1]
    per_step = x_refs[0].shape[0]
    step = pl.program_id(0)
    me = me_ref[0]
    spacing = blocks * ROWS
    share = out_refs[0].shape[1] // moments

    def section(s, carry):
        number = step * per_step + s
        wind = Wind(ux_ref[number], uy_ref[number], blocks)

        def code(u, j):
            spot = (wind.row(u, 0, ROWS - 1) * blocks + wind.block(j)) * TILE
            return code_ref[pl.ds(pl.multiple_of(spot, TILE), TILE), :]

        for low in range(0, moments, together):
            some = range(low, min(moments, low + together))
            chains = []
            for m in some:
                tiles = [
                    [
                        x_refs[m][
                            s,
                            pl.ds(
                                wind.block(j) * ROWS + wind.row(u, 0, ROWS - 1),
                                TILE,
                                stride=spacing,
                            ),
                            :,
                        ]
                        for j in range(blocks)
                    ]
                    for u in range(ROWS)
                ]
                chains.append((wind, tiles, code, inflow_ref[number, base + m]))
            for m, state in zip(some, substeps(chains)):
                keep(wind, state, packed.at[m])
        for m in range(moments):
            scatter(
                packed.at[m],
                me,
                [(out, (s, slice(m * share, (m + 1) * share))) for out in out_refs],
            )
        return carry

    lax.fori_loop(0, per_step, section, 0)


def outer_kernel(
    some, halos, blocks, together, me_ref, odd_ref, ux_ref, uy_ref, inflow_ref, _,
    near_ref, far_ref, code_ref, *rest
):
    count = len(some)
    x_refs, rest = rest[:count], rest[count:]
    halo_refs, rest = rest[: sum(halos)], rest[sum(halos) :]
    out_refs, (codes, packed) = rest[:-2], rest[-2:]
    per_step = x_refs[0].shape[0]
    step = pl.program_id(0)
    me = me_ref[0]
    odd = odd_ref[0]
    spacing = blocks * ROWS
    edge = SUB * blocks * TILE
    share = packed.shape[1] // len(out_refs)

    @pl.when(odd == 1)
    def _():
        codes[:edge] = near_ref[1]
        codes[edge : 2 * edge] = far_ref[0]

    @pl.when(odd != 1)
    def _():
        codes[:edge] = far_ref[1]
        codes[edge : 2 * edge] = near_ref[0]

    codes[2 * edge :] = code_ref[...]

    def sections(turn, carry):
        for m in range(count):
            chains = []
            for i in range(together):
                s = turn * together + i
                number = step * per_step + s
                wind = Wind(ux_ref[number], uy_ref[number], blocks)
                outside = jnp.where(wind.positive_x, 0, edge)
                second = jnp.logical_xor(wind.positive_x, odd == 1)
                first_halo = sum(halos[:m])

                def code(u, j, wind=wind, outside=outside):
                    if u < SUB:
                        spot = outside + (wind.row(u, 0, SUB - 1) * blocks + wind.block(j)) * TILE
                    else:
                        row = wind.row(u, -SUB, ROWS + SUB - 1)
                        spot = 2 * edge + (row * blocks + wind.block(j)) * TILE
                    return codes[pl.ds(pl.multiple_of(spot, TILE), TILE), :]

                tiles = []
                for u in range(ROWS):
                    row = []
                    for j in range(blocks):
                        if u < SUB:
                            spot = (wind.row(u, 0, SUB - 1) * blocks + wind.block(j)) * TILE
                            spot = pl.ds(pl.multiple_of(spot, TILE), TILE)
                            tile = halo_refs[first_halo][s, spot, :]
                            if halos[m] == 2:
                                tile = jnp.where(second, halo_refs[first_halo + 1][s, spot, :], tile)
                        else:
                            start = wind.block(j) * ROWS + wind.row(u, -SUB, ROWS + SUB - 1)
                            tile = x_refs[m][s, pl.ds(start, TILE, stride=spacing), :]
                        row.append(tile)
                    tiles.append(row)
                chains.append((wind, tiles, code, inflow_ref[number, some[m]]))
            for i, (chain, state) in enumerate(zip(chains, substeps(chains))):
                keep(chain[0], state, packed.at[m * together + i])
            for i in range(together):
                number = step * per_step + turn * together + i
                spot = (number, slice(m * share, (m + 1) * share))
                scatter(packed.at[m * together + i], me, [(out, spot) for out in out_refs])
        return carry

    lax.fori_loop(0, per_step // together, sections, 0)
    if some[0] == 0:

        @pl.when(step == 0)
        def _():
            size = out_refs[0].shape[1]
            for number in range(size):
                line = jnp.full((1, LANES), ux_ref[number], F32)
                for out in out_refs:
                    out[size, number : number + 1, :] = line


def split_dot(weights, values):
    high = values.astype(BF16)
    rest = (values - high.astype(F32)).astype(BF16)
    return jnp.dot(
        weights, jnp.concatenate([high, rest, high], axis=0), preferred_element_type=F32
    )


def couple_kernel(first, groups, group_size, blocks, *refs):
    me_ref, rate_ref, share_ref, thermal_ref = refs[:4]
    refs = refs[4:]
    sign_refs, inner, outer = refs[:groups], refs[groups : 2 * groups], refs[2 * groups : 3 * groups]
    refs = refs[3 * groups :]
    if first:
        kernel_ref, spray_ref, gas_ref, merge_ref, *scratch = refs
    else:
        merge_ref, _, _, _, spray_ref, gas_ref, *scratch = refs
    rest, made, total = scratch
    me = me_ref[0]
    sections = groups * group_size
    size = ROWS * blocks
    half = size // 2
    thermal = [thermal_ref[:half, :], thermal_ref[half:, :]]
    gas = tuple(jnp.zeros((half, LANES), F32) for _ in thermal)
    for k in range(groups):

        def section(s, sums, k=k):
            number = (me ^ k) * group_size + s
            flip = jnp.broadcast_to(sign_refs[k][0, pl.ds(s, 1), :], (half, LANES)) > 0.0
            rate = rate_ref[number]
            one, two = inner[k][s], outer[k][s]
            result = []
            for i, moved in enumerate((jnp.where(flip, two, one), jnp.where(flip, one, two))):
                evaporated = (rate * thermal[i]) * moved
                result.append(sums[i] + evaporated)
                rest[pl.ds(pl.multiple_of(number * size + i * half, half), half), :] = moved - evaporated
            return tuple(result)

        gas = lax.fori_loop(0, group_size, section, gas, unroll=4)
    for i in range(2):
        total[i * half : (i + 1) * half, :] = gas[i]
    for block in range(blocks):
        gas_ref[0, :, block * LANES : (block + 1) * LANES] = total[pl.ds(block, ROWS, stride=blocks), :]
    for row in range(ROWS):
        spots = [pl.ds(row * blocks + block, sections, stride=size) for block in range(blocks)]
        cells = jnp.concatenate([rest[spot, :] for spot in spots], axis=1)
        if first:
            merge = split_dot(kernel_ref[...], cells)
            merge_ref[row] = merge
        else:
            merge = merge_ref[row]
        flux = cells * merge
        result = cells - flux + split_dot(share_ref[...], flux)
        for block, spot in enumerate(spots):
            made[spot, :] = result[:, block * LANES : (block + 1) * LANES]

    def write(s, carry):
        for block in range(blocks):
            spray_ref[s, 0, :, block * LANES : (block + 1) * LANES] = made[
                pl.ds(s * size + block, ROWS, stride=blocks), :
            ]
        return carry

    lax.fori_loop(0, sections, write, 0, unroll=8)


def params(**more):
    return pltpu.CompilerParams(vmem_limit_bytes=VMEM_LIMIT, **more)


def split_weights(weights):
    high = lax.reduce_precision(weights, 8, 7)
    return jnp.concatenate([high, high, weights - high], axis=1).astype(BF16)


def shards(
    droplet_integrals,
    flow_number_lengthwise,
    flow_number_crosswise,
    inflow_boundary_integrals,
    boundary_wall_indicator,
    inflow_indicator,
    collision_coefficient,
    collision_target_share,
    evaporation_speed_stepwise,
    thermal_factor,
):
    x, ux, uy = droplet_integrals, flow_number_lengthwise, flow_number_crosswise
    group_size, moments, rows, columns = x.shape
    groups = lax.axis_size("sec")
    slabs = lax.axis_size("space")
    sections = groups * group_size
    width = columns // groups
    blocks = columns // (TILE * LANES)
    size = columns // LANES * ROWS
    share_size = size // 2 // groups
    assert rows == ROWS and slabs % 2 == 0 and TILE % groups == 0

    me = lax.axis_index("sec").astype(jnp.int32).reshape(1)
    odd = (lax.axis_index("space") % 2).astype(jnp.int32).reshape(1)

    swap = [(i, i ^ 1) for i in range(slabs)]
    outward = [(i, i + 2) for i in range(0, slabs - 2, 2)] + [(i, i - 2) for i in range(3, slabs, 2)]
    inward = [(j, i) for i, j in outward]

    smem = pl.BlockSpec(memory_space=pltpu.SMEM)
    anywhere = pl.BlockSpec(memory_space=pl.ANY)
    cells = stacked(x).reshape(group_size, moments * size, LANES)

    def moment_specs(per_step, some):
        return [
            pl.BlockSpec((per_step, size, LANES), lambda g, moment=moment: (g, moment, 0))
            for moment in some
        ]

    def exchange(parts):
        return [parts[0]] + [
            lax.ppermute(parts[k], "sec", [(i, i ^ k) for i in range(groups)])
            for k in range(1, groups)
        ]

    edge = SUB * blocks * TILE
    flat = pl.BlockSpec((size, LANES), lambda g: (0, 0))

    def after(value, *events):
        return lax.optimization_barrier((value, *events))[0]

    def select(outs, last):
        some = sum(outs, ())
        coded = last is None
        per_step = group_size // 2
        operands = [ux] + [cells] * len(some)
        out_shape = [
            jax.ShapeDtypeStruct((group_size + 2 * (held[0] == 0), len(held) * edge, LANES), F32)
            for held in outs
        ]
        out_specs = [pl.BlockSpec(shape.shape, lambda g: (0, 0, 0)) for shape in out_shape]
        scratch = []
        if coded:
            in_specs = [pl.BlockSpec(memory_space=pltpu.HBM)] * 2
            operands += [stacked(boundary_wall_indicator), stacked(inflow_indicator)]
            out_specs.append(flat)
            out_shape.append(jax.ShapeDtypeStruct((size, LANES), F32))
            scratch = [pltpu.VMEM((size, LANES), jnp.int32)] * 2 + [pltpu.SemaphoreType.DMA((2,))]
        else:
            in_specs = [anywhere]
            operands += [last]
        return pl.pallas_call(
            functools.partial(select_kernel, tuple(len(held) for held in outs), blocks),
            grid=(group_size // per_step,),
            in_specs=[smem] + moment_specs(per_step, some) + in_specs,
            out_specs=out_specs,
            out_shape=out_shape,
            scratch_shapes=scratch,
            compiler_params=params(),
            cost_estimate=pl.CostEstimate(
                flops=x.size, bytes_accessed=x.size * 6 * len(some) // moments, transcendentals=0
            ),
            name="select_upwind_rows",
        )(*operands)

    def transport_inner(some, last):
        per_step = 4
        count = len(some)
        return pl.pallas_call(
            functools.partial(inner_kernel, some[0], count, blocks, TOGETHER_INNER),
            grid=(group_size // per_step,),
            in_specs=[smem] * 4 + [anywhere, flat] + moment_specs(per_step, some),
            out_specs=[pl.BlockSpec((per_step, count * share_size, LANES), lambda g: (g, 0, 0))]
            * groups,
            out_shape=[jax.ShapeDtypeStruct((group_size, count * share_size, LANES), F32)] * groups,
            scratch_shapes=[pltpu.VMEM((count, size // 2, LANES), F32)],
            compiler_params=params(),
            cost_estimate=pl.CostEstimate(
                flops=x.size * 4 * count, bytes_accessed=x.size * count, transcendentals=0
            ),
            name="transport_inner_rows",
        )(me, ux, uy, inflow_boundary_integrals, last, code, *[cells] * count)

    def transport_outer(some, halos, last):
        per_step = group_size // 2
        count = len(some)
        length = group_size + (some[0] == 0)
        line = pl.BlockSpec((2, edge, LANES), lambda g: (group_size // 2, 0, 0))
        flat_halos = sum(halos, ())
        return pl.pallas_call(
            functools.partial(
                outer_kernel, some, tuple(len(h) for h in halos), blocks, TOGETHER_OUTER
            ),
            grid=(group_size // per_step,),
            in_specs=[smem] * 5
            + [anywhere, line, line, flat]
            + moment_specs(per_step, some)
            + [pl.BlockSpec((per_step, edge, LANES), lambda g: (g, 0, 0))] * len(flat_halos),
            out_specs=[pl.BlockSpec((length, count * share_size, LANES), lambda g: (0, 0, 0))]
            * groups,
            out_shape=[jax.ShapeDtypeStruct((length, count * share_size, LANES), F32)] * groups,
            scratch_shapes=[
                pltpu.VMEM((2 * edge + size, LANES), F32),
                pltpu.VMEM((count * TOGETHER_OUTER, size // 2, LANES), F32),
            ],
            compiler_params=params(),
            cost_estimate=pl.CostEstimate(
                flops=x.size * 4 * count, bytes_accessed=x.size * 2 * count, transcendentals=0
            ),
            name="transport_outer_rows",
        )(
            me, odd, ux, uy, inflow_boundary_integrals, last, *code_halos, code,
            *[cells] * count, *flat_halos
        )

    def relay(own, far, count, last):
        return pl.pallas_call(
            functools.partial(relay_kernel, count),
            grid=(1,),
            in_specs=[smem, smem, anywhere]
            + [pl.BlockSpec(own.shape, lambda g: (0, 0, 0))] * 2,
            out_specs=[pl.BlockSpec((group_size, edge, LANES), lambda g: (0, 0, 0))] * count,
            out_shape=[jax.ShapeDtypeStruct((group_size, edge, LANES), F32)] * count,
            compiler_params=params(),
            cost_estimate=pl.CostEstimate(
                flops=0, bytes_accessed=own.size * 12, transcendentals=0
            ),
            name="relay_upwind_rows",
        )(odd, ux, last, own, far)

    def swapped(array):
        return lax.ppermute(array, "space", swap)

    def hopped(array, pairs):
        return lax.ppermute(array, "space", pairs)

    chosen_0, chosen_34, code = select([(0,), (3, 4)], None)
    near_0 = swapped(chosen_0)
    far_34 = hopped(chosen_34, inward)
    inner_a = transport_inner((0, 1), chosen_0)
    chosen_1, chosen_2 = select([(1,), (2,)], inner_a[0])
    near_1 = swapped(chosen_1)
    far_0 = hopped(near_0, outward)
    code_halos = (near_0, far_0)
    inner_b = transport_inner((2, 3, 4), chosen_1)
    sent_a = exchange(inner_a)
    near_2 = swapped(after(chosen_2, near_0))
    far_1 = hopped(near_1, outward)
    relayed_3, relayed_4 = relay(chosen_34, far_34, 2, inner_b[0])
    near_3 = swapped(after(relayed_3, near_1))
    far_2 = hopped(near_2, outward)
    near_4 = swapped(after(relayed_4, near_2))
    sent_b = exchange([after(part, *sent_a) for part in inner_b])
    outer_0 = transport_outer((0,), ((near_0, far_0),), after(relayed_3, *sent_a))
    sent_0 = exchange([after(part, *sent_b) for part in outer_0])
    outer_1 = transport_outer((1,), ((near_1, far_1),), after(outer_0[0], *sent_b))
    sent_1 = exchange([after(part, *sent_0) for part in outer_1])
    outer_23 = transport_outer(
        (2, 3), ((near_2, far_2), (near_3,)), after(outer_1[0], *sent_0)
    )
    sent_23 = exchange([after(part, *sent_1) for part in outer_23])
    outer_4 = transport_outer((4,), ((near_4,),), after(outer_23[0], *sent_1))
    sent_4 = exchange(outer_4)
    plan = (
        ((0,), sent_a, 0, sent_0, outer_1[0]),
        ((1,), sent_a, 1, sent_1, outer_23[0]),
        ((2, 3), sent_b, 0, sent_23, outer_4[0]),
        ((4,), sent_b, 2, sent_4, outer_4[0]),
    )

    share = split_weights(collision_target_share)
    kernel = split_weights(collision_coefficient)
    step_width = blocks * LANES
    steps = width // step_width
    step_size = ROWS * blocks
    thermal = thermal_factor.reshape(ROWS, steps, blocks, LANES).swapaxes(0, 1)
    thermal = thermal.reshape(steps * step_size, LANES)
    spray_type = jax.ShapeDtypeStruct((sections, moments, rows, width), F32)
    gas_type = jax.ShapeDtypeStruct((moments, rows, width), F32)
    merge_type = jax.ShapeDtypeStruct((rows, sections, width), F32)
    merge_spec = pl.BlockSpec((rows, sections, step_width), lambda m, j: (0, 0, j))
    spray = gas = merge = None
    for some, inner, base, outer, last in plan:
        first = some[0] == 0

        def part(lead, length, offset):
            return pl.BlockSpec(
                (lead, length, LANES), lambda m, j, offset=offset: (0, (offset + m) * steps + j, 0)
            )

        in_specs = (
            [smem] * 2
            + [
                pl.BlockSpec(share.shape, lambda m, j: (0, 0)),
                pl.BlockSpec((step_size, LANES), lambda m, j: (j, 0)),
            ]
            + [pl.BlockSpec((1, share_size, LANES), lambda m, j: (group_size, 0, 0))] * groups
            + [part(group_size, step_size // 2, base)] * groups
            + [part(group_size, step_size // 2, 0)] * groups
        )
        operands = [me, evaporation_speed_stepwise, share, thermal]
        operands += list(sent_0) + list(inner) + list(outer)
        out_specs = [
            pl.BlockSpec(
                (sections, 1, rows, step_width), lambda m, j, some=some: (0, some[0] + m, 0, j)
            ),
            pl.BlockSpec((1, rows, step_width), lambda m, j, some=some: (some[0] + m, 0, j)),
        ]
        out_shape = [spray_type, gas_type]
        aliases = {}
        if first:
            in_specs.append(pl.BlockSpec(kernel.shape, lambda m, j: (0, 0)))
            operands.append(kernel)
            out_specs.append(merge_spec)
            out_shape.append(merge_type)
        else:
            aliases = {len(operands) + 1: 0, len(operands) + 2: 1}
            in_specs += [merge_spec, anywhere, anywhere, anywhere]
            operands += [merge, spray, gas, last]
        made = pl.pallas_call(
            functools.partial(couple_kernel, first, groups, group_size, blocks),
            grid=(len(some), steps),
            in_specs=in_specs,
            out_specs=out_specs,
            out_shape=out_shape,
            input_output_aliases=aliases,
            scratch_shapes=[pltpu.VMEM((sections * step_size, LANES), F32)] * 2
            + [pltpu.VMEM((step_size, LANES), F32)],
            compiler_params=params(),
            cost_estimate=pl.CostEstimate(
                flops=sections * rows * width * sections * 2 * len(some),
                bytes_accessed=sections * rows * width * 12 * len(some),
                transcendentals=0,
            ),
            name="couple_sections",
        )(*operands)
        if first:
            spray, gas, merge = made
        else:
            spray, gas = made
    return spray, gas


def solution(mesh):
    return jax.shard_map(
        shards,
        mesh=mesh,
        in_specs=(
            P("sec", None, "space", None),
            P("sec"),
            P("sec"),
            P("sec", None),
            P("space", None),
            P("space", None),
            P(),
            P(),
            P(),
            P("space", "sec"),
        ),
        out_specs=(P(None, None, "space", "sec"), P(None, "space", "sec")),
        check_vma=False,
    )
```

```python
import functools

import jax
import jax.numpy as jnp
from jax import lax
from jax.experimental import pallas as pl
from jax.experimental.pallas import tpu as pltpu
from jax.sharding import PartitionSpec as P

SUB = 4
ROWS = 2 * SUB
LANES = 128
TILE = 8
F32 = jnp.float32
BF16 = jnp.bfloat16
CHAINS = 10
SORT_LIMIT = 44 * 1024 * 1024
SELECT_LIMIT = 50 * 1024 * 1024
VMEM_LIMIT = 8 * 1024 * 1024


def stacked(array):
    *lead, rows, columns = array.shape
    tiles = columns // LANES
    array = array.reshape(*lead, rows, tiles, LANES)
    return jnp.swapaxes(array, -3, -2).reshape(*lead, rows * tiles, LANES)


class Scalars:
    def __init__(self, place_ref, ux_ref, uy_ref, inflow_ref):
        self.me, self.odd = place_ref[0], place_ref[1]
        self.ux_ref, self.uy_ref, self.inflow_ref = ux_ref, uy_ref, inflow_ref

    def ux(self, s):
        return self.ux_ref[s]

    def wind(self, s, blocks):
        return Wind(self.ux_ref[s], self.uy_ref[s], blocks)

    def inflow(self, s, moment):
        return self.inflow_ref[moment, s]


def sublane(shape=(TILE, LANES)):
    return lax.broadcasted_iota(jnp.int32, shape, 0)


class Wind:
    def __init__(self, speed_x, speed_y, blocks):
        self.a, self.b = jnp.abs(speed_x), jnp.abs(speed_y)
        self.own = 1.0 - self.a - self.b
        self.blocks = blocks
        self.positive_x = speed_x > 0.0
        self.positive_y = speed_y > 0.0
        lane = lax.broadcasted_iota(jnp.int32, (TILE, LANES), 1)
        self.lane_shift = jnp.where(self.positive_y, 1, LANES - 1).astype(jnp.int32)
        self.band_shift = jnp.where(self.positive_y, 1, TILE - 1).astype(jnp.int32)
        self.edge = lane == jnp.where(self.positive_y, 0, LANES - 1)
        self.border = sublane() == jnp.where(self.positive_y, 0, TILE - 1)

    def row(self, u, first, last):
        return jnp.where(self.positive_x, first + u, last - u)

    def block(self, j):
        return jnp.where(self.positive_y, j, self.blocks - 1 - j)


def substeps(chains):
    states = [chain[1] for chain in chains]
    for step in range(1, SUB + 1):
        fresh = []
        for (wind, _, code, value), state in zip(chains, states):
            rows = [None] * step
            for u in range(step, ROWS):
                turned = [pltpu.roll(tile, wind.lane_shift, axis=1) for tile in state[u]]
                wrap = pltpu.roll(turned[-1], wind.band_shift, axis=0)
                behind = [jnp.where(wind.border, 0.0, wrap)] + turned[:-1]
                tiles = []
                for j, tile in enumerate(state[u]):
                    side = jnp.where(wind.edge, behind[j], turned[j])
                    moved = wind.own * tile + wind.a * state[u - 1][j] + wind.b * side
                    kind = code(u, j)
                    tiles.append(jnp.where(kind < 0.0, moved, kind * value))
                rows.append(tiles)
            fresh.append(rows)
        states = fresh
    return states


def keep(wind, state, packed):
    blocks = wind.blocks
    for u in range(SUB, ROWS):
        row = wind.row(u, -SUB, ROWS - 1)
        for j, tile in enumerate(state[u]):
            packed[pl.ds(row * blocks + wind.block(j), TILE, stride=SUB * blocks), :] = tile


def scatter(packed, me, outs):
    share = packed.shape[0] // len(outs)
    for k, (out, spot) in enumerate(outs):
        start = pl.multiple_of((me ^ k) * share, share)
        out[spot] = packed[pl.ds(start, share), :]


def select_kernel(outs, blocks, ux_ref, *refs):
    count = sum(outs)
    x_refs, kind_ref, out_refs, code_ref = refs[:count], refs[count], refs[count + 1 : -1], refs[-1]
    per_step, size = x_refs[0].shape[:2]
    step = pl.program_id(0)
    edge = size // 2

    def section(s, carry):
        number = step * per_step + s
        first = jnp.where(ux_ref[number] > 0.0, SUB, 0)
        sources = iter(x_refs)
        for held, out_ref in zip(outs, out_refs):
            for i in range(held):
                x_ref = next(sources)
                for row in range(SUB):
                    for block in range(blocks):
                        spot = i * edge + (row * blocks + block) * TILE
                        source = pl.ds(block * ROWS + first + row, TILE, stride=blocks * ROWS)
                        out_ref[number, spot : spot + TILE, :] = x_ref[s, source, :]
        return carry

    lax.fori_loop(0, per_step, section, 0, unroll=2)

    @pl.when(step == 0)
    def _():
        last = out_refs[0].shape[0] - 2
        for row in range(ROWS):
            for block in range(blocks):
                spot = (row * blocks + block) * TILE
                source = pl.ds(block * ROWS + row, TILE, stride=blocks * ROWS)
                code_ref[spot : spot + TILE, :] = kind_ref[source, :]
        for i in range(2):
            out_refs[0][last + i] = code_ref[i * edge : (i + 1) * edge, :]


def sort_kernel(outs, blocks, ux_ref, x_ref, *refs):
    count = len(refs) - len(outs)
    cell_refs, out_refs = refs[:count], refs[count:]
    per_step = x_ref.shape[0]
    step = pl.program_id(0)
    size = cell_refs[0].shape[1]
    edge = size // 2

    def sort(source, target):
        for band in range(TILE):
            for block in range(blocks):
                tile = source((band * blocks + block) * ROWS)
                target[pl.ds(block * TILE + band, ROWS, stride=blocks * TILE), :] = tile

    def section(s, carry):
        number = step * per_step + s
        first = pl.multiple_of(jnp.where(ux_ref[number] > 0.0, edge, 0), edge)
        for m, cell_ref in enumerate(cell_refs):

            def source(spot, m=m):
                return x_ref[s, m * size + spot : m * size + spot + ROWS, :]

            sort(source, cell_ref.at[number])
        for held, out_ref in zip(outs, out_refs):
            for i, m in enumerate(held):
                out_ref[number, i * edge : (i + 1) * edge, :] = cell_refs[m][
                    number, pl.ds(first, edge), :
                ]
        return carry

    lax.fori_loop(0, per_step, section, 0)


def relay_kernel(total, place_ref, ux_ref, uy_ref, inflow_ref, _, own_ref, far_ref, *out_refs):
    scalars = Scalars(place_ref, ux_ref, uy_ref, inflow_ref)
    size = own_ref.shape[1] // len(out_refs)

    def relay(s, stays):
        def copy(source):
            for i, out_ref in enumerate(out_refs):
                out_ref[s] = source[s, i * size : (i + 1) * size, :]

        pl.when(stays)(lambda: copy(own_ref))
        pl.when(jnp.logical_not(stays))(lambda: copy(far_ref))

    def section(s, carry):
        relay(s, (scalars.ux(s) > 0.0) != (scalars.odd == 1))
        return carry

    lax.fori_loop(0, total, section, 0)
    if own_ref.shape[0] > total:
        relay(total, scalars.odd == 1)
        relay(total + 1, scalars.odd != 1)


def inner_kernel(
    some, blocks, together, place_ref, ux_ref, uy_ref, inflow_ref, _, code_ref, *rest
):
    count = len(some)
    cell_refs, out_refs, packed = rest[:count], rest[count:-1], rest[-1]
    total = cell_refs[0].shape[0]
    scalars = Scalars(place_ref, ux_ref, uy_ref, inflow_ref)
    share = packed.shape[1] // len(out_refs)

    def sections(turn, carry):
        chains, places = [], []
        for i in range(together):
            s = turn * together + i
            wind = scalars.wind(s, blocks)

            def spot(u, j, wind=wind):
                row = wind.row(u, 0, ROWS - 1)
                return pl.ds(pl.multiple_of((row * blocks + wind.block(j)) * TILE, TILE), TILE)

            def code(u, j, spot=spot):
                return code_ref[spot(u, j), :]

            for m, cell_ref in enumerate(cell_refs):
                tiles = [[cell_ref[s, spot(u, j), :] for j in range(blocks)] for u in range(ROWS)]
                chains.append((wind, tiles, code, scalars.inflow(s, some[m])))
                places.append((s, slice(m * share, (m + 1) * share)))
        for c, (chain, state) in enumerate(zip(chains, substeps(chains))):
            keep(chain[0], state, packed.at[c])
        for c, place in enumerate(places):
            scatter(packed.at[c], scalars.me, [(out, place) for out in out_refs])
        return carry

    lax.fori_loop(0, total // together, sections, 0)


def outer_kernel(
    some, halos, starts, blocks, together, place_ref, ux_ref, uy_ref, inflow_ref, _,
    edge_ref, code_ref, *rest
):
    count = len(some)
    cell_refs, rest = rest[:count], rest[count:]
    halo_refs, rest = rest[: sum(halos)], rest[sum(halos) :]
    out_refs, (codes, packed) = rest[:-2], rest[-2:]
    total = cell_refs[0].shape[0]
    scalars = Scalars(place_ref, ux_ref, uy_ref, inflow_ref)
    me, odd = scalars.me, scalars.odd
    edge = SUB * blocks * TILE
    share = packed.shape[1] // len(out_refs)
    last = edge_ref.shape[0] - 2
    codes[:edge] = edge_ref[last + 1]
    codes[edge : 2 * edge] = edge_ref[last]
    codes[2 * edge :] = code_ref[...]

    def sections(turn, carry):
        chains, places = [], []
        for i in range(together):
            s = turn * together + i
            wind = scalars.wind(s, blocks)
            outside = jnp.where(wind.positive_x, 0, edge)
            second = jnp.logical_xor(wind.positive_x, odd == 1)

            def spot(u, j, wind=wind):
                if u < SUB:
                    row = wind.row(u, 0, SUB - 1)
                else:
                    row = wind.row(u, -SUB, ROWS + SUB - 1)
                return (row * blocks + wind.block(j)) * TILE

            def code(u, j, spot=spot, outside=outside):
                at = spot(u, j) + (outside if u < SUB else 2 * edge)
                return codes[pl.ds(pl.multiple_of(at, TILE), TILE), :]

            for m, cell_ref in enumerate(cell_refs):
                held = halo_refs[sum(halos[:m]) : sum(halos[: m + 1])]
                skip = starts[m] * edge
                tiles = []
                for u in range(ROWS):
                    row = []
                    for j in range(blocks):
                        at = spot(u, j) + (skip if u < SUB else 0)
                        at = pl.ds(pl.multiple_of(at, TILE), TILE)
                        if u >= SUB:
                            tile = cell_ref[s, at, :]
                        elif len(held) == 2:
                            tile = jnp.where(second, held[1][s, at, :], held[0][s, at, :])
                        else:
                            tile = held[0][s, at, :]
                        row.append(tile)
                    tiles.append(row)
                chains.append((wind, tiles, code, scalars.inflow(s, some[m])))
                places.append((s, slice(m * share, (m + 1) * share)))
        for c, (chain, state) in enumerate(zip(chains, substeps(chains))):
            keep(chain[0], state, packed.at[c])
        for c, place in enumerate(places):
            scatter(packed.at[c], me, [(out, place) for out in out_refs])
        return carry

    lax.fori_loop(0, total // together, sections, 0)
    if some[0] == 0:
        for s in range(total):
            line = jnp.full((1, LANES), scalars.ux(s), F32)
            for out in out_refs:
                out[total, s : s + 1, :] = line


def split_dot(weights, values):
    high = values.astype(BF16)
    rest = (values - high.astype(F32)).astype(BF16)
    return jnp.dot(
        weights, jnp.concatenate([high, rest, high], axis=0), preferred_element_type=F32
    )


def couple_kernel(first, base, groups, group_size, blocks, *refs):
    me_ref, rate_ref, share_ref, thermal_ref = refs[:4]
    refs = refs[4:]
    sign_refs, inner, outer = refs[:groups], refs[groups : 2 * groups], refs[2 * groups : 3 * groups]
    refs = refs[3 * groups :]
    if first:
        kernel_ref, spray_ref, gas_ref, merge_ref, *scratch = refs
    else:
        merge_ref, _, _, _, spray_ref, gas_ref, *scratch = refs
    rest, total = scratch
    spray_rows = spray_ref.reshape(spray_ref.shape[0] * spray_ref.shape[1], LANES)
    me = me_ref[0]
    moment, step = pl.program_id(0), pl.program_id(1)
    sections = groups * group_size
    size = ROWS * blocks
    half = size // 2
    steps = thermal_ref.shape[0] // size
    inner_spot = pl.ds(pl.multiple_of(((base + moment) * steps + step) * half, half), half)
    outer_spot = pl.ds(pl.multiple_of((moment * steps + step) * half, half), half)
    columns = pl.ds(pl.multiple_of(step * blocks * LANES, LANES), blocks * LANES)
    thermal = [
        thermal_ref[pl.ds(pl.multiple_of(step * size + i * half, half), half), :] for i in range(2)
    ]
    gas = tuple(jnp.zeros((half, LANES), F32) for _ in thermal)
    for k in range(groups):

        def section(s, sums, k=k):
            number = (me ^ k) * group_size + s
            flip = jnp.broadcast_to(sign_refs[k][group_size, pl.ds(s, 1), :], (half, LANES)) > 0.0
            rate = rate_ref[number]
            one, two = inner[k][s, inner_spot, :], outer[k][s, outer_spot, :]
            result = []
            for i, moved in enumerate((jnp.where(flip, two, one), jnp.where(flip, one, two))):
                evaporated = (rate * thermal[i]) * moved
                result.append(sums[i] + evaporated)
                rest[pl.ds(i * half * sections + number, half, stride=sections), :] = moved - evaporated
            return tuple(result)

        gas = lax.fori_loop(0, group_size, section, gas, unroll=4)
    for i in range(2):
        total[i * half : (i + 1) * half, :] = gas[i]
    for block in range(blocks):
        gas_ref[0, :, block * LANES : (block + 1) * LANES] = total[pl.ds(block, ROWS, stride=blocks), :]
    for row in range(ROWS):
        spots = [(row * blocks + block) * sections for block in range(blocks)]
        cells = jnp.concatenate([rest[spot : spot + sections, :] for spot in spots], axis=1)
        if first:
            merge = split_dot(kernel_ref[...], cells)
            merge_ref[row, :, columns] = merge
        else:
            merge = merge_ref[row, :, columns]
        flux = cells * merge
        result = cells - flux + split_dot(share_ref[...], flux)
        for block in range(blocks):
            spray_rows[pl.ds(block * ROWS + row, sections, stride=size), :] = result[
                :, block * LANES : (block + 1) * LANES
            ]


def params(limit=VMEM_LIMIT):
    return pltpu.CompilerParams(vmem_limit_bytes=limit)


def split_weights(weights):
    high = lax.reduce_precision(weights, 8, 7)
    return jnp.concatenate([high, high, weights - high], axis=1).astype(BF16)


def shards(
    droplet_integrals,
    flow_number_lengthwise,
    flow_number_crosswise,
    inflow_boundary_integrals,
    boundary_wall_indicator,
    inflow_indicator,
    collision_coefficient,
    collision_target_share,
    evaporation_speed_stepwise,
    thermal_factor,
):
    x, ux, uy = droplet_integrals, flow_number_lengthwise, flow_number_crosswise
    group_size, moments, rows, columns = x.shape
    groups = lax.axis_size("sec")
    slabs = lax.axis_size("space")
    sections = groups * group_size
    width = columns // groups
    blocks = columns // (TILE * LANES)
    size = columns // LANES * ROWS
    share_size = size // 2 // groups
    assert rows == ROWS and slabs % 2 == 0 and TILE % groups == 0

    swap = [(i, i ^ 1) for i in range(slabs)]
    outward = [(i, i + 2) for i in range(0, slabs - 2, 2)] + [(i, i - 2) for i in range(3, slabs, 2)]
    inward = [(j, i) for i, j in outward]

    smem = pl.BlockSpec(memory_space=pltpu.SMEM)
    anywhere = pl.BlockSpec(memory_space=pl.ANY)
    cells = stacked(x).reshape(group_size, moments * size, LANES)

    vmem = pl.BlockSpec(memory_space=pltpu.VMEM)
    edge = SUB * blocks * TILE
    place = jnp.stack([lax.axis_index("sec"), lax.axis_index("space") % 2]).astype(jnp.int32)

    def send(parts, first, last, *events):
        return [
            lax.ppermute(after(parts[k], *events), "sec", [(i, i ^ k) for i in range(groups)])
            for k in range(first, last)
        ]

    def after(value, *events):
        return lax.optimization_barrier((value, *events))[0]

    def select(outs):
        some = sum(outs, ())
        per_step = group_size // 2
        shapes = [
            (group_size + 2 * (i == 0), len(held) * edge, LANES) for i, held in enumerate(outs)
        ] + [(size, LANES)]
        kind = jnp.where(inflow_indicator > 0, 1.0, -1.0)
        kind = jnp.where(boundary_wall_indicator > 0, 0.0, kind).astype(F32)
        return pl.pallas_call(
            functools.partial(select_kernel, tuple(len(held) for held in outs), blocks),
            grid=(group_size // per_step,),
            in_specs=[smem]
            + [
                pl.BlockSpec((per_step, size, LANES), lambda g, moment=moment: (g, moment, 0))
                for moment in some
            ]
            + [vmem],
            out_specs=[vmem] * len(shapes),
            out_shape=[jax.ShapeDtypeStruct(shape, F32) for shape in shapes],
            compiler_params=params(SELECT_LIMIT),
            cost_estimate=cost(len(some), x.size),
            name="select_upwind_rows",
        )(after(ux, place), *[cells] * len(some), stacked(kind))

    def sort(outs, last):
        per_step = group_size // 4
        shapes = [(group_size, size, LANES)] * moments
        shapes += [(group_size, len(held) * edge, LANES) for held in outs]
        made = pl.pallas_call(
            functools.partial(sort_kernel, outs, blocks),
            grid=(group_size // per_step,),
            in_specs=[
                smem, pl.BlockSpec((per_step, moments * size, LANES), lambda g: (g, 0, 0))
            ],
            out_specs=[vmem] * len(shapes),
            out_shape=[jax.ShapeDtypeStruct(shape, F32) for shape in shapes],
            compiler_params=params(SORT_LIMIT),
            cost_estimate=cost(moments, x.size),
            name="sort_cells",
        )(after(ux, last), cells)
        return made[:moments], made[moments:]

    def cost(count, amount):
        return pl.CostEstimate(
            flops=amount * count, bytes_accessed=amount * count, transcendentals=0
        )

    def whole(kernel, name, last, operands, out_shapes, scratch=(), count=1):
        return pl.pallas_call(
            kernel,
            in_specs=[smem] * 4 + [anywhere] + [vmem] * len(operands),
            out_specs=[vmem] * len(out_shapes),
            out_shape=[jax.ShapeDtypeStruct(shape, F32) for shape in out_shapes],
            scratch_shapes=list(scratch),
            compiler_params=params(),
            cost_estimate=cost(count, x.size),
            name=name,
        )(place, ux, uy, inflow_boundary_integrals.T, last, *operands)

    def together(some):
        count = 1
        while 2 * count * len(some) <= CHAINS and group_size % (2 * count) == 0:
            count *= 2
        return count

    def transport_inner(some, last):
        return whole(
            functools.partial(inner_kernel, some, blocks, together(some)),
            "transport_inner_rows",
            last,
            [code, *[own[moment] for moment in some]],
            [(group_size, len(some) * share_size, LANES)] * groups,
            [pltpu.VMEM((together(some) * len(some), size // 2, LANES), F32)],
            count=len(some),
        )

    def transport_outer(some, halos, last, starts=None):
        return whole(
            functools.partial(
                outer_kernel,
                some,
                tuple(len(h) for h in halos),
                starts or (0,) * len(some),
                blocks,
                together(some),
            ),
            "transport_outer_rows",
            last,
            [near_0, code, *[own[moment] for moment in some], *sum(halos, ())],
            [(group_size + (some[0] == 0), len(some) * share_size, LANES)] * groups,
            [
                pltpu.VMEM((2 * edge + size, LANES), F32),
                pltpu.VMEM((together(some) * len(some), size // 2, LANES), F32),
            ],
            count=len(some),
        )

    def relay(own, far, count, last):
        return whole(
            functools.partial(relay_kernel, group_size),
            "relay_upwind_rows",
            last,
            [own, far],
            [(own.shape[0], own.shape[1] // count, LANES)] * count,
        )

    def swapped(array):
        return lax.ppermute(array, "space", swap)

    def hopped(array, pairs):
        return lax.ppermute(array, "space", pairs)

    share = split_weights(collision_target_share)
    kernel = split_weights(collision_coefficient)
    step_width = blocks * LANES
    steps = width // step_width
    step_size = ROWS * blocks
    thermal = thermal_factor.reshape(ROWS, steps, blocks, LANES).swapaxes(0, 1)
    thermal = thermal.reshape(steps * step_size, LANES)
    spray_type = jax.ShapeDtypeStruct((sections, moments * steps * step_size, LANES), F32)
    gas_type = jax.ShapeDtypeStruct((moments, rows, width), F32)
    merge_type = jax.ShapeDtypeStruct((rows, sections, width), F32)
    made = {}

    def couple(some, inner, base, outer, last):
        first = some[0] == 0

        in_specs = [smem] * 2 + [vmem] * (2 + 3 * groups)
        operands = [place, evaporation_speed_stepwise, share, thermal]
        operands += list(made.setdefault("sign", outer)) + list(inner) + list(outer)
        out_specs = [
            pl.BlockSpec(
                (sections, step_size, LANES), lambda m, j: (0, (some[0] + m) * steps + j, 0)
            ),
            pl.BlockSpec((1, rows, step_width), lambda m, j: (some[0] + m, 0, j)),
        ]
        out_shape = [spray_type, gas_type]
        aliases = {}
        if first:
            in_specs.append(vmem)
            operands.append(kernel)
            out_specs.append(vmem)
            out_shape.append(merge_type)
        else:
            aliases = {len(operands) + 1: 0, len(operands) + 2: 1}
            in_specs += [vmem, anywhere, anywhere, anywhere]
            operands += [made["merge"], made["spray"], made["gas"], last]
        result = pl.pallas_call(
            functools.partial(couple_kernel, first, base, groups, group_size, blocks),
            grid=(len(some), steps),
            in_specs=in_specs,
            out_specs=out_specs,
            out_shape=out_shape,
            input_output_aliases=aliases,
            scratch_shapes=[
                pltpu.VMEM((sections * step_size, LANES), F32),
                pltpu.VMEM((step_size, LANES), F32),
            ],
            compiler_params=params(),
            cost_estimate=pl.CostEstimate(
                flops=sections * rows * width * sections * 2 * len(some),
                bytes_accessed=sections * rows * width * 12 * len(some),
                transcendentals=0,
            ),
            name="couple_sections",
        )(*operands)
        made.update(zip(("spray", "gas", "merge"), result))

    chosen_0, chosen_12, code = select(((0,), (1, 2)))
    near_12 = swapped(chosen_12)
    far_0 = hopped(chosen_0, inward)
    own, (chosen_34,) = sort(((3, 4),), code)
    far_34 = hopped(chosen_34, inward)
    inner = transport_inner(tuple(range(moments)), chosen_34)
    far_in = send(inner, 2, groups)
    (relayed_0,) = relay(chosen_0, far_0, 1, inner[0])
    near_0 = swapped(relayed_0)
    far_12 = hopped(after(near_12, relayed_0), outward)
    (relayed_34,) = relay(chosen_34, far_34, 1, after(relayed_0, near_0))
    near_34 = swapped(relayed_34)
    outer_0 = transport_outer((0,), ((near_0,),), after(relayed_34, *far_in))
    far_of_0 = send(outer_0, 2, groups, *far_in)
    pair_in = send(inner, 1, 2, outer_0[0])
    pair_of_0 = send(outer_0, 1, 2, far_12, *pair_in)
    outer_12 = transport_outer(
        (1, 2), ((near_12, far_12), (near_12, far_12)), outer_0[0], (0, 1)
    )
    far_of_12 = send(outer_12, 2, groups, near_34)
    outer_3 = transport_outer((3,), ((near_34,),), after(outer_12[0], *far_of_0), (0,))
    far_of_3 = send(outer_3, 2, groups)
    pair_of_12 = send(outer_12, 1, 2, *pair_of_0)
    sent = [inner[0], *pair_in, *far_in]
    couple((0,), sent, 0, [outer_0[0], *pair_of_0, *far_of_0], outer_3[0])
    outer_4 = transport_outer((4,), ((near_34,),), made["merge"], (1,))
    pair_of_3 = send(outer_3, 1, 2, *pair_of_12)
    sent_4 = [outer_4[0]] + send(outer_4, 1, groups)
    couple((1, 2), sent, 1, [outer_12[0], *pair_of_12, *far_of_12], outer_4[0])
    couple((3,), sent, 3, [outer_3[0], *pair_of_3, *far_of_3], outer_4[0])
    couple((4,), sent, 4, sent_4, outer_4[0])
    spray = jnp.swapaxes(
        made["spray"].reshape(sections, moments, width // LANES, rows, LANES), 2, 3
    )
    return spray.reshape(sections, moments, rows, width), made["gas"]


def solution(mesh):
    return jax.shard_map(
        shards,
        mesh=mesh,
        in_specs=(
            P("sec", None, "space", None),
            P("sec"),
            P("sec"),
            P("sec", None),
            P("space", None),
            P("space", None),
            P(),
            P(),
            P(),
            P("space", "sec"),
        ),
        out_specs=(P(None, None, "space", "sec"), P(None, "space", "sec")),
        check_vma=False,
    )
```

```python
import functools

import jax
import jax.numpy as jnp
from jax import lax
from jax.experimental import pallas as pl
from jax.experimental.pallas import tpu as pltpu
from jax.sharding import PartitionSpec as P

SUB = 4
ROWS = 2 * SUB
LANES = 128
TILE = 8
F32 = jnp.float32
BF16 = jnp.bfloat16
CHAINS = 10
SORT_LIMIT = 44 * 1024 * 1024
SELECT_LIMIT = 50 * 1024 * 1024
VMEM_LIMIT = 8 * 1024 * 1024


def stacked(array):
    *lead, rows, columns = array.shape
    tiles = columns // LANES
    array = array.reshape(*lead, rows, tiles, LANES)
    return jnp.swapaxes(array, -3, -2).reshape(*lead, rows * tiles, LANES)


class Scalars:
    def __init__(self, place_ref, ux_ref, uy_ref, inflow_ref):
        self.me, self.odd = place_ref[0], place_ref[1]
        self.ux_ref, self.uy_ref, self.inflow_ref = ux_ref, uy_ref, inflow_ref

    def ux(self, s):
        return self.ux_ref[s]

    def wind(self, s, blocks):
        return Wind(self.ux_ref[s], self.uy_ref[s], blocks)

    def inflow(self, s, moment):
        return self.inflow_ref[moment, s]


def sublane(shape=(TILE, LANES)):
    return lax.broadcasted_iota(jnp.int32, shape, 0)


class Wind:
    def __init__(self, speed_x, speed_y, blocks):
        self.a, self.b = jnp.abs(speed_x), jnp.abs(speed_y)
        self.own = 1.0 - self.a - self.b
        self.blocks = blocks
        self.positive_x = speed_x > 0.0
        self.positive_y = speed_y > 0.0
        lane = lax.broadcasted_iota(jnp.int32, (TILE, LANES), 1)
        self.lane_shift = jnp.where(self.positive_y, 1, LANES - 1).astype(jnp.int32)
        self.band_shift = jnp.where(self.positive_y, 1, TILE - 1).astype(jnp.int32)
        self.edge = lane == jnp.where(self.positive_y, 0, LANES - 1)
        self.border = sublane() == jnp.where(self.positive_y, 0, TILE - 1)

    def row(self, u, first, last):
        return jnp.where(self.positive_x, first + u, last - u)

    def block(self, j):
        return jnp.where(self.positive_y, j, self.blocks - 1 - j)


def substeps(chains):
    states = [chain[1] for chain in chains]
    for step in range(1, SUB + 1):
        fresh = []
        for (wind, _, code, value), state in zip(chains, states):
            rows = [None] * step
            for u in range(step, ROWS):
                turned = [pltpu.roll(tile, wind.lane_shift, axis=1) for tile in state[u]]
                wrap = pltpu.roll(turned[-1], wind.band_shift, axis=0)
                behind = [jnp.where(wind.border, 0.0, wrap)] + turned[:-1]
                tiles = []
                for j, tile in enumerate(state[u]):
                    side = jnp.where(wind.edge, behind[j], turned[j])
                    moved = wind.own * tile + wind.a * state[u - 1][j] + wind.b * side
                    kind = code(u, j)
                    tiles.append(jnp.where(kind < 0.0, moved, kind * value))
                rows.append(tiles)
            fresh.append(rows)
        states = fresh
    return states


def keep(wind, state, packed):
    blocks = wind.blocks
    for u in range(SUB, ROWS):
        row = wind.row(u, -SUB, ROWS - 1)
        for j, tile in enumerate(state[u]):
            packed[pl.ds(row * blocks + wind.block(j), TILE, stride=SUB * blocks), :] = tile


def scatter(packed, me, outs):
    share = packed.shape[0] // len(outs)
    for k, (out, spot) in enumerate(outs):
        start = pl.multiple_of((me ^ k) * share, share)
        out[spot] = packed[pl.ds(start, share), :]


def select_kernel(outs, blocks, ux_ref, *refs):
    count = sum(outs)
    x_refs, kind_ref, out_refs, code_ref = refs[:count], refs[count], refs[count + 1 : -1], refs[-1]
    per_step, size = x_refs[0].shape[:2]
    step = pl.program_id(0)
    edge = size // 2

    def section(s, carry):
        number = step * per_step + s
        first = jnp.where(ux_ref[number] > 0.0, SUB, 0)
        sources = iter(x_refs)
        for held, out_ref in zip(outs, out_refs):
            for i in range(held):
                x_ref = next(sources)
                for row in range(SUB):
                    for block in range(blocks):
                        spot = i * edge + (row * blocks + block) * TILE
                        source = pl.ds(block * ROWS + first + row, TILE, stride=blocks * ROWS)
                        out_ref[number, spot : spot + TILE, :] = x_ref[s, source, :]
        return carry

    lax.fori_loop(0, per_step, section, 0, unroll=2)

    @pl.when(step == 0)
    def _():
        last = out_refs[0].shape[0] - 2
        for row in range(ROWS):
            for block in range(blocks):
                spot = (row * blocks + block) * TILE
                source = pl.ds(block * ROWS + row, TILE, stride=blocks * ROWS)
                code_ref[spot : spot + TILE, :] = kind_ref[source, :]
        for i in range(2):
            out_refs[0][last + i] = code_ref[i * edge : (i + 1) * edge, :]


def sort_kernel(outs, blocks, ux_ref, x_ref, *refs):
    count = len(refs) - len(outs)
    cell_refs, out_refs = refs[:count], refs[count:]
    per_step = x_ref.shape[0]
    step = pl.program_id(0)
    size = cell_refs[0].shape[1]
    edge = size // 2

    def sort(source, target):
        for band in range(TILE):
            for block in range(blocks):
                tile = source((band * blocks + block) * ROWS)
                target[pl.ds(block * TILE + band, ROWS, stride=blocks * TILE), :] = tile

    def section(s, carry):
        number = step * per_step + s
        first = pl.multiple_of(jnp.where(ux_ref[number] > 0.0, edge, 0), edge)
        for m, cell_ref in enumerate(cell_refs):

            def source(spot, m=m):
                return x_ref[s, m * size + spot : m * size + spot + ROWS, :]

            sort(source, cell_ref.at[number])
        for held, out_ref in zip(outs, out_refs):
            for i, m in enumerate(held):
                out_ref[number, i * edge : (i + 1) * edge, :] = cell_refs[m][
                    number, pl.ds(first, edge), :
                ]
        return carry

    lax.fori_loop(0, per_step, section, 0)


def relay_kernel(total, place_ref, ux_ref, uy_ref, inflow_ref, _, own_ref, far_ref, *out_refs):
    scalars = Scalars(place_ref, ux_ref, uy_ref, inflow_ref)
    size = own_ref.shape[1] // len(out_refs)

    def relay(s, stays):
        def copy(source):
            for i, out_ref in enumerate(out_refs):
                out_ref[s] = source[s, i * size : (i + 1) * size, :]

        pl.when(stays)(lambda: copy(own_ref))
        pl.when(jnp.logical_not(stays))(lambda: copy(far_ref))

    def section(s, carry):
        relay(s, (scalars.ux(s) > 0.0) != (scalars.odd == 1))
        return carry

    lax.fori_loop(0, total, section, 0)
    if own_ref.shape[0] > total:
        relay(total, scalars.odd == 1)
        relay(total + 1, scalars.odd != 1)


def inner_kernel(
    some, blocks, together, place_ref, ux_ref, uy_ref, inflow_ref, _, code_ref, *rest
):
    count = len(some)
    cell_refs, out_refs, packed = rest[:count], rest[count:-1], rest[-1]
    total = cell_refs[0].shape[0]
    scalars = Scalars(place_ref, ux_ref, uy_ref, inflow_ref)
    share = packed.shape[1] // len(out_refs)

    def sections(turn, carry):
        chains, places = [], []
        for i in range(together):
            s = turn * together + i
            wind = scalars.wind(s, blocks)

            def spot(u, j, wind=wind):
                row = wind.row(u, 0, ROWS - 1)
                return pl.ds(pl.multiple_of((row * blocks + wind.block(j)) * TILE, TILE), TILE)

            def code(u, j, spot=spot):
                return code_ref[spot(u, j), :]

            for m, cell_ref in enumerate(cell_refs):
                tiles = [[cell_ref[s, spot(u, j), :] for j in range(blocks)] for u in range(ROWS)]
                chains.append((wind, tiles, code, scalars.inflow(s, some[m])))
                places.append((s, slice(m * share, (m + 1) * share)))
        for c, (chain, state) in enumerate(zip(chains, substeps(chains))):
            keep(chain[0], state, packed.at[c])
        for c, place in enumerate(places):
            scatter(packed.at[c], scalars.me, [(out, place) for out in out_refs])
        return carry

    lax.fori_loop(0, total // together, sections, 0)


def outer_kernel(
    some, halos, starts, blocks, together, place_ref, ux_ref, uy_ref, inflow_ref, _,
    edge_ref, code_ref, *rest
):
    count = len(some)
    cell_refs, rest = rest[:count], rest[count:]
    halo_refs, rest = rest[: sum(halos)], rest[sum(halos) :]
    out_refs, (codes, packed) = rest[:-2], rest[-2:]
    total = cell_refs[0].shape[0]
    scalars = Scalars(place_ref, ux_ref, uy_ref, inflow_ref)
    me, odd = scalars.me, scalars.odd
    edge = SUB * blocks * TILE
    share = packed.shape[1] // len(out_refs)
    last = edge_ref.shape[0] - 2
    codes[:edge] = edge_ref[last + 1]
    codes[edge : 2 * edge] = edge_ref[last]
    codes[2 * edge :] = code_ref[...]

    def sections(turn, carry):
        chains, places = [], []
        for i in range(together):
            s = turn * together + i
            wind = scalars.wind(s, blocks)
            outside = jnp.where(wind.positive_x, 0, edge)
            second = jnp.logical_xor(wind.positive_x, odd == 1)

            def spot(u, j, wind=wind):
                if u < SUB:
                    row = wind.row(u, 0, SUB - 1)
                else:
                    row = wind.row(u, -SUB, ROWS + SUB - 1)
                return (row * blocks + wind.block(j)) * TILE

            def code(u, j, spot=spot, outside=outside):
                at = spot(u, j) + (outside if u < SUB else 2 * edge)
                return codes[pl.ds(pl.multiple_of(at, TILE), TILE), :]

            for m, cell_ref in enumerate(cell_refs):
                held = halo_refs[sum(halos[:m]) : sum(halos[: m + 1])]
                skip = starts[m] * edge
                tiles = []
                for u in range(ROWS):
                    row = []
                    for j in range(blocks):
                        at = spot(u, j) + (skip if u < SUB else 0)
                        at = pl.ds(pl.multiple_of(at, TILE), TILE)
                        if u >= SUB:
                            tile = cell_ref[s, at, :]
                        elif len(held) == 2:
                            tile = jnp.where(second, held[1][s, at, :], held[0][s, at, :])
                        else:
                            tile = held[0][s, at, :]
                        row.append(tile)
                    tiles.append(row)
                chains.append((wind, tiles, code, scalars.inflow(s, some[m])))
                places.append((s, slice(m * share, (m + 1) * share)))
        for c, (chain, state) in enumerate(zip(chains, substeps(chains))):
            keep(chain[0], state, packed.at[c])
        for c, place in enumerate(places):
            scatter(packed.at[c], me, [(out, place) for out in out_refs])
        return carry

    lax.fori_loop(0, total // together, sections, 0)
    if some[0] == 0:
        for s in range(total):
            line = jnp.full((1, LANES), scalars.ux(s), F32)
            for out in out_refs:
                out[total, s : s + 1, :] = line


def split_dot(weights, values):
    high = values.astype(BF16)
    rest = (values - high.astype(F32)).astype(BF16)
    return jnp.dot(
        weights, jnp.concatenate([high, rest, high], axis=0), preferred_element_type=F32
    )


def couple_kernel(first, base, groups, group_size, blocks, *refs):
    me_ref, rate_ref, share_ref, thermal_ref = refs[:4]
    refs = refs[4:]
    sign_refs, inner, outer = refs[:groups], refs[groups : 2 * groups], refs[2 * groups : 3 * groups]
    refs = refs[3 * groups :]
    if first:
        kernel_ref, spray_ref, gas_ref, merge_ref, *scratch = refs
    else:
        merge_ref, _, _, _, spray_ref, gas_ref, *scratch = refs
    rest, total = scratch
    spray_rows = spray_ref.reshape(spray_ref.shape[0] * spray_ref.shape[1], LANES)
    me = me_ref[0]
    moment, step = pl.program_id(0), pl.program_id(1)
    sections = groups * group_size
    size = ROWS * blocks
    half = size // 2
    steps = thermal_ref.shape[0] // size
    inner_spot = pl.ds(pl.multiple_of(((base + moment) * steps + step) * half, half), half)
    outer_spot = pl.ds(pl.multiple_of((moment * steps + step) * half, half), half)
    columns = pl.ds(pl.multiple_of(step * blocks * LANES, LANES), blocks * LANES)
    thermal = [
        thermal_ref[pl.ds(pl.multiple_of(step * size + i * half, half), half), :] for i in range(2)
    ]
    gas = tuple(jnp.zeros((half, LANES), F32) for _ in thermal)
    for k in range(groups):

        def section(s, sums, k=k):
            number = (me ^ k) * group_size + s
            flip = jnp.broadcast_to(sign_refs[k][group_size, pl.ds(s, 1), :], (half, LANES)) > 0.0
            rate = rate_ref[number]
            one, two = inner[k][s, inner_spot, :], outer[k][s, outer_spot, :]
            result = []
            for i, moved in enumerate((jnp.where(flip, two, one), jnp.where(flip, one, two))):
                evaporated = (rate * thermal[i]) * moved
                result.append(sums[i] + evaporated)
                rest[pl.ds(i * half * sections + number, half, stride=sections), :] = moved - evaporated
            return tuple(result)

        gas = lax.fori_loop(0, group_size, section, gas, unroll=4)
    for i in range(2):
        total[i * half : (i + 1) * half, :] = gas[i]
    for block in range(blocks):
        gas_ref[0, :, block * LANES : (block + 1) * LANES] = total[pl.ds(block, ROWS, stride=blocks), :]
    for row in range(ROWS):
        spots = [(row * blocks + block) * sections for block in range(blocks)]
        cells = jnp.concatenate([rest[spot : spot + sections, :] for spot in spots], axis=1)
        if first:
            merge = split_dot(kernel_ref[...], cells)
            merge_ref[row, :, columns] = merge
        else:
            merge = merge_ref[row, :, columns]
        flux = cells * merge
        result = cells - flux + split_dot(share_ref[...], flux)
        for block in range(blocks):
            spray_rows[pl.ds(block * ROWS + row, sections, stride=size), :] = result[
                :, block * LANES : (block + 1) * LANES
            ]


def params(limit=VMEM_LIMIT):
    return pltpu.CompilerParams(vmem_limit_bytes=limit)


def split_weights(weights):
    high = lax.reduce_precision(weights, 8, 7)
    return jnp.concatenate([high, high, weights - high], axis=1).astype(BF16)


def shards(
    droplet_integrals,
    flow_number_lengthwise,
    flow_number_crosswise,
    inflow_boundary_integrals,
    boundary_wall_indicator,
    inflow_indicator,
    collision_coefficient,
    collision_target_share,
    evaporation_speed_stepwise,
    thermal_factor,
):
    x, ux, uy = droplet_integrals, flow_number_lengthwise, flow_number_crosswise
    group_size, moments, rows, columns = x.shape
    groups = lax.axis_size("sec")
    slabs = lax.axis_size("space")
    sections = groups * group_size
    width = columns // groups
    blocks = columns // (TILE * LANES)
    size = columns // LANES * ROWS
    share_size = size // 2 // groups
    assert rows == ROWS and slabs % 2 == 0 and TILE % groups == 0

    swap = [(i, i ^ 1) for i in range(slabs)]
    outward = [(i, i + 2) for i in range(0, slabs - 2, 2)] + [(i, i - 2) for i in range(3, slabs, 2)]
    inward = [(j, i) for i, j in outward]

    smem = pl.BlockSpec(memory_space=pltpu.SMEM)
    anywhere = pl.BlockSpec(memory_space=pl.ANY)
    cells = stacked(x).reshape(group_size, moments * size, LANES)

    vmem = pl.BlockSpec(memory_space=pltpu.VMEM)
    edge = SUB * blocks * TILE
    place = jnp.stack([lax.axis_index("sec"), lax.axis_index("space") % 2]).astype(jnp.int32)

    def send(parts, first, last, *events):
        return [
            lax.ppermute(after(parts[k], *events), "sec", [(i, i ^ k) for i in range(groups)])
            for k in range(first, last)
        ]

    def after(value, *events):
        return lax.optimization_barrier((value, *events))[0]

    def select(outs):
        some = sum(outs, ())
        per_step = group_size // 2
        shapes = [
            (group_size + 2 * (i == 0), len(held) * edge, LANES) for i, held in enumerate(outs)
        ] + [(size, LANES)]
        kind = jnp.where(inflow_indicator > 0, 1.0, -1.0)
        kind = jnp.where(boundary_wall_indicator > 0, 0.0, kind).astype(F32)
        return pl.pallas_call(
            functools.partial(select_kernel, tuple(len(held) for held in outs), blocks),
            grid=(group_size // per_step,),
            in_specs=[smem]
            + [
                pl.BlockSpec((per_step, size, LANES), lambda g, moment=moment: (g, moment, 0))
                for moment in some
            ]
            + [vmem],
            out_specs=[vmem] * len(shapes),
            out_shape=[jax.ShapeDtypeStruct(shape, F32) for shape in shapes],
            compiler_params=params(SELECT_LIMIT),
            cost_estimate=cost(len(some), x.size),
            name="select_upwind_rows",
        )(after(ux, place), *[cells] * len(some), stacked(kind))

    def sort(outs, last):
        per_step = group_size // 4
        shapes = [(group_size, size, LANES)] * moments
        shapes += [(group_size, len(held) * edge, LANES) for held in outs]
        made = pl.pallas_call(
            functools.partial(sort_kernel, outs, blocks),
            grid=(group_size // per_step,),
            in_specs=[
                smem, pl.BlockSpec((per_step, moments * size, LANES), lambda g: (g, 0, 0))
            ],
            out_specs=[vmem] * len(shapes),
            out_shape=[jax.ShapeDtypeStruct(shape, F32) for shape in shapes],
            compiler_params=params(SORT_LIMIT),
            cost_estimate=cost(moments, x.size),
            name="sort_cells",
        )(after(ux, last), cells)
        return made[:moments], made[moments:]

    def cost(count, amount):
        return pl.CostEstimate(
            flops=amount * count, bytes_accessed=amount * count, transcendentals=0
        )

    def whole(kernel, name, last, operands, out_shapes, scratch=(), count=1):
        return pl.pallas_call(
            kernel,
            in_specs=[smem] * 4 + [anywhere] + [vmem] * len(operands),
            out_specs=[vmem] * len(out_shapes),
            out_shape=[jax.ShapeDtypeStruct(shape, F32) for shape in out_shapes],
            scratch_shapes=list(scratch),
            compiler_params=params(),
            cost_estimate=cost(count, x.size),
            name=name,
        )(place, ux, uy, inflow_boundary_integrals.T, last, *operands)

    def together(some):
        count = 1
        while 2 * count * len(some) <= CHAINS and group_size % (2 * count) == 0:
            count *= 2
        return count

    def transport_inner(some, last):
        return whole(
            functools.partial(inner_kernel, some, blocks, together(some)),
            "transport_inner_rows",
            last,
            [code, *[own[moment] for moment in some]],
            [(group_size, len(some) * share_size, LANES)] * groups,
            [pltpu.VMEM((together(some) * len(some), size // 2, LANES), F32)],
            count=len(some),
        )

    def transport_outer(some, halos, last, starts=None):
        return whole(
            functools.partial(
                outer_kernel,
                some,
                tuple(len(h) for h in halos),
                starts or (0,) * len(some),
                blocks,
                together(some),
            ),
            "transport_outer_rows",
            last,
            [near_0, code, *[own[moment] for moment in some], *sum(halos, ())],
            [(group_size + (some[0] == 0), len(some) * share_size, LANES)] * groups,
            [
                pltpu.VMEM((2 * edge + size, LANES), F32),
                pltpu.VMEM((together(some) * len(some), size // 2, LANES), F32),
            ],
            count=len(some),
        )

    def relay(own, far, count, last):
        return whole(
            functools.partial(relay_kernel, group_size),
            "relay_upwind_rows",
            last,
            [own, far],
            [(own.shape[0], own.shape[1] // count, LANES)] * count,
        )

    def swapped(array):
        return lax.ppermute(array, "space", swap)

    def hopped(array, pairs):
        return lax.ppermute(array, "space", pairs)

    share = split_weights(collision_target_share)
    kernel = split_weights(collision_coefficient)
    step_width = blocks * LANES
    steps = width // step_width
    step_size = ROWS * blocks
    thermal = thermal_factor.reshape(ROWS, steps, blocks, LANES).swapaxes(0, 1)
    thermal = thermal.reshape(steps * step_size, LANES)
    spray_type = jax.ShapeDtypeStruct((sections, moments * steps * step_size, LANES), F32)
    gas_type = jax.ShapeDtypeStruct((moments, rows, width), F32)
    merge_type = jax.ShapeDtypeStruct((rows, sections, width), F32)
    made = {}

    def couple(some, inner, base, outer, last):
        first = some[0] == 0

        in_specs = [smem] * 2 + [vmem] * (2 + 3 * groups)
        operands = [place, evaporation_speed_stepwise, share, after(thermal, last) if first else thermal]
        operands += list(made.setdefault("sign", outer)) + list(inner) + list(outer)
        out_specs = [
            pl.BlockSpec(
                (sections, step_size, LANES), lambda m, j: (0, (some[0] + m) * steps + j, 0)
            ),
            pl.BlockSpec((1, rows, step_width), lambda m, j: (some[0] + m, 0, j)),
        ]
        out_shape = [spray_type, gas_type]
        aliases = {}
        if first:
            in_specs.append(vmem)
            operands.append(kernel)
            out_specs.append(vmem)
            out_shape.append(merge_type)
        else:
            aliases = {len(operands) + 1: 0, len(operands) + 2: 1}
            in_specs += [vmem, anywhere, anywhere, anywhere]
            operands += [made["merge"], made["spray"], made["gas"], last]
        result = pl.pallas_call(
            functools.partial(couple_kernel, first, base, groups, group_size, blocks),
            grid=(len(some), steps),
            in_specs=in_specs,
            out_specs=out_specs,
            out_shape=out_shape,
            input_output_aliases=aliases,
            scratch_shapes=[
                pltpu.VMEM((sections * step_size, LANES), F32),
                pltpu.VMEM((step_size, LANES), F32),
            ],
            compiler_params=params(),
            cost_estimate=pl.CostEstimate(
                flops=sections * rows * width * sections * 2 * len(some),
                bytes_accessed=sections * rows * width * 12 * len(some),
                transcendentals=0,
            ),
            name="couple_sections",
        )(*operands)
        made.update(zip(("spray", "gas", "merge"), result))

    chosen_0, chosen_12, code = select(((0,), (1, 2)))
    near_12 = swapped(chosen_12)
    far_0 = hopped(chosen_0, inward)
    own, (chosen_34,) = sort(((3, 4),), code)
    far_34 = hopped(chosen_34, inward)
    inner = transport_inner(tuple(range(moments)), chosen_34)
    far_in = send(inner, 2, groups)
    (relayed_0,) = relay(chosen_0, far_0, 1, inner[0])
    near_0 = swapped(relayed_0)
    far_12 = hopped(after(near_12, relayed_0), outward)
    (relayed_34,) = relay(chosen_34, far_34, 1, after(relayed_0, near_0))
    near_34 = swapped(relayed_34)
    outer_0 = transport_outer((0,), ((near_0,),), after(relayed_34, far_in[-1]))
    far_of_0 = [part for k in range(2, groups) for part in send(outer_0, k, k + 1, far_in[k - 2])]
    pair_in = send(inner, 1, 2, outer_0[0], far_in[0])
    pair_of_0 = send(outer_0, 1, 2, *pair_in)
    outer_12 = transport_outer(
        (1, 2), ((near_12, far_12), (near_12, far_12)), after(outer_0[0], *far_of_0), (0, 1)
    )
    far_of_12 = send(outer_12, 2, 3) + send(outer_12, 3, groups, near_34)
    sent = [inner[0], *pair_in, *far_in]
    couple((0,), sent, 0, [outer_0[0], *pair_of_0, *far_of_0], far_of_12[0])
    outer_3 = transport_outer((3,), ((near_34,),), made["merge"], (0,))
    far_of_3 = send(outer_3, 2, groups)
    pair_of_12 = send(outer_12, 1, 2, near_34, *pair_of_0)
    outer_4 = transport_outer((4,), ((near_34,),), outer_3[0], (1,))
    pair_of_3 = send(outer_3, 1, 2, *pair_of_12)
    sent_4 = [outer_4[0]] + send(outer_4, 1, 2, *pair_of_3) + send(outer_4, 2, groups, *far_of_12)
    couple((1, 2), sent, 1, [outer_12[0], *pair_of_12, *far_of_12], outer_4[0])
    couple((3,), sent, 3, [outer_3[0], *pair_of_3, *far_of_3], outer_4[0])
    couple((4,), sent, 4, sent_4, outer_4[0])
    spray = jnp.swapaxes(
        made["spray"].reshape(sections, moments, width // LANES, rows, LANES), 2, 3
    )
    return spray.reshape(sections, moments, rows, width), made["gas"]


def solution(mesh):
    return jax.shard_map(
        shards,
        mesh=mesh,
        in_specs=(
            P("sec", None, "space", None),
            P("sec"),
            P("sec"),
            P("sec", None),
            P("space", None),
            P("space", None),
            P(),
            P(),
            P(),
            P("space", "sec"),
        ),
        out_specs=(P(None, None, "space", "sec"), P(None, "space", "sec")),
        check_vma=False,
    )
```

```python
import functools

import jax
import jax.numpy as jnp
from jax import lax
from jax.experimental import pallas as pl
from jax.experimental.pallas import tpu as pltpu
from jax.sharding import PartitionSpec as P

SUB = 4
ROWS = 2 * SUB
LANES = 128
TILE = 8
F32 = jnp.float32
BF16 = jnp.bfloat16
CHAINS = 10
SORT_LIMIT = 44 * 1024 * 1024
SELECT_LIMIT = 50 * 1024 * 1024
VMEM_LIMIT = 8 * 1024 * 1024


def stacked(array):
    *lead, rows, columns = array.shape
    tiles = columns // LANES
    array = array.reshape(*lead, rows, tiles, LANES)
    return jnp.swapaxes(array, -3, -2).reshape(*lead, rows * tiles, LANES)


class Scalars:
    def __init__(self, place_ref, ux_ref, uy_ref, inflow_ref):
        self.me, self.odd = place_ref[0], place_ref[1]
        self.ux_ref, self.uy_ref, self.inflow_ref = ux_ref, uy_ref, inflow_ref

    def ux(self, s):
        return self.ux_ref[s]

    def wind(self, s, blocks):
        return Wind(self.ux_ref[s], self.uy_ref[s], blocks)

    def inflow(self, s, moment):
        return self.inflow_ref[moment, s]


def sublane(shape=(TILE, LANES)):
    return lax.broadcasted_iota(jnp.int32, shape, 0)


class Wind:
    def __init__(self, speed_x, speed_y, blocks):
        self.a, self.b = jnp.abs(speed_x), jnp.abs(speed_y)
        self.own = 1.0 - self.a - self.b
        self.blocks = blocks
        self.positive_x = speed_x > 0.0
        self.positive_y = speed_y > 0.0
        lane = lax.broadcasted_iota(jnp.int32, (TILE, LANES), 1)
        self.lane_shift = jnp.where(self.positive_y, 1, LANES - 1).astype(jnp.int32)
        self.band_shift = jnp.where(self.positive_y, 1, TILE - 1).astype(jnp.int32)
        self.edge = lane == jnp.where(self.positive_y, 0, LANES - 1)
        self.border = sublane() == jnp.where(self.positive_y, 0, TILE - 1)

    def row(self, u, first, last):
        return jnp.where(self.positive_x, first + u, last - u)

    def block(self, j):
        return jnp.where(self.positive_y, j, self.blocks - 1 - j)


def substeps(chains):
    states = [chain[1] for chain in chains]
    for step in range(1, SUB + 1):
        fresh = []
        for (wind, _, code, value), state in zip(chains, states):
            rows = [None] * step
            for u in range(step, ROWS):
                turned = [pltpu.roll(tile, wind.lane_shift, axis=1) for tile in state[u]]
                wrap = pltpu.roll(turned[-1], wind.band_shift, axis=0)
                behind = [jnp.where(wind.border, 0.0, wrap)] + turned[:-1]
                tiles = []
                for j, tile in enumerate(state[u]):
                    side = jnp.where(wind.edge, behind[j], turned[j])
                    moved = wind.own * tile + wind.a * state[u - 1][j] + wind.b * side
                    kind = code(u, j)
                    tiles.append(jnp.where(kind < 0.0, moved, kind * value))
                rows.append(tiles)
            fresh.append(rows)
        states = fresh
    return states


def keep(wind, state, packed):
    blocks = wind.blocks
    for u in range(SUB, ROWS):
        row = wind.row(u, -SUB, ROWS - 1)
        for j, tile in enumerate(state[u]):
            packed[pl.ds(row * blocks + wind.block(j), TILE, stride=SUB * blocks), :] = tile


def scatter(packed, me, outs):
    share = packed.shape[0] // len(outs)
    for k, (out, spot) in enumerate(outs):
        start = pl.multiple_of((me ^ k) * share, share)
        out[spot] = packed[pl.ds(start, share), :]


def select_kernel(outs, blocks, ux_ref, *refs):
    count = sum(outs)
    x_refs, kind_ref, out_refs, code_ref = refs[:count], refs[count], refs[count + 1 : -1], refs[-1]
    per_step, size = x_refs[0].shape[:2]
    step = pl.program_id(0)
    edge = size // 2

    def section(s, carry):
        number = step * per_step + s
        first = jnp.where(ux_ref[number] > 0.0, SUB, 0)
        sources = iter(x_refs)
        for held, out_ref in zip(outs, out_refs):
            for i in range(held):
                x_ref = next(sources)
                for row in range(SUB):
                    for block in range(blocks):
                        spot = i * edge + (row * blocks + block) * TILE
                        source = pl.ds(block * ROWS + first + row, TILE, stride=blocks * ROWS)
                        out_ref[number, spot : spot + TILE, :] = x_ref[s, source, :]
        return carry

    lax.fori_loop(0, per_step, section, 0, unroll=2)

    @pl.when(step == 0)
    def _():
        last = out_refs[0].shape[0] - 2
        for row in range(ROWS):
            for block in range(blocks):
                spot = (row * blocks + block) * TILE
                source = pl.ds(block * ROWS + row, TILE, stride=blocks * ROWS)
                code_ref[spot : spot + TILE, :] = kind_ref[source, :]
        for i in range(2):
            out_refs[0][last + i] = code_ref[i * edge : (i + 1) * edge, :]


def sort_kernel(outs, blocks, ux_ref, x_ref, *refs):
    count = len(refs) - len(outs)
    cell_refs, out_refs = refs[:count], refs[count:]
    per_step = x_ref.shape[0]
    step = pl.program_id(0)
    size = cell_refs[0].shape[1]
    edge = size // 2

    def sort(source, target):
        for band in range(TILE):
            for block in range(blocks):
                tile = source((band * blocks + block) * ROWS)
                target[pl.ds(block * TILE + band, ROWS, stride=blocks * TILE), :] = tile

    def section(s, carry):
        number = step * per_step + s
        first = pl.multiple_of(jnp.where(ux_ref[number] > 0.0, edge, 0), edge)
        for m, cell_ref in enumerate(cell_refs):

            def source(spot, m=m):
                return x_ref[s, m * size + spot : m * size + spot + ROWS, :]

            sort(source, cell_ref.at[number])
        for held, out_ref in zip(outs, out_refs):
            for i, m in enumerate(held):
                out_ref[number, i * edge : (i + 1) * edge, :] = cell_refs[m][
                    number, pl.ds(first, edge), :
                ]
        return carry

    lax.fori_loop(0, per_step, section, 0)


def relay_kernel(total, place_ref, ux_ref, uy_ref, inflow_ref, _, own_ref, far_ref, *out_refs):
    scalars = Scalars(place_ref, ux_ref, uy_ref, inflow_ref)
    size = own_ref.shape[1] // len(out_refs)

    def relay(s, stays):
        def copy(source):
            for i, out_ref in enumerate(out_refs):
                out_ref[s] = source[s, i * size : (i + 1) * size, :]

        pl.when(stays)(lambda: copy(own_ref))
        pl.when(jnp.logical_not(stays))(lambda: copy(far_ref))

    def section(s, carry):
        relay(s, (scalars.ux(s) > 0.0) != (scalars.odd == 1))
        return carry

    lax.fori_loop(0, total, section, 0)
    if own_ref.shape[0] > total:
        relay(total, scalars.odd == 1)
        relay(total + 1, scalars.odd != 1)


def inner_kernel(
    some, blocks, together, place_ref, ux_ref, uy_ref, inflow_ref, _, code_ref, *rest
):
    count = len(some)
    cell_refs, out_refs, packed = rest[:count], rest[count:-1], rest[-1]
    total = cell_refs[0].shape[0]
    scalars = Scalars(place_ref, ux_ref, uy_ref, inflow_ref)
    share = packed.shape[1] // len(out_refs)

    def sections(turn, carry):
        chains, places = [], []
        for i in range(together):
            s = turn * together + i
            wind = scalars.wind(s, blocks)

            def spot(u, j, wind=wind):
                row = wind.row(u, 0, ROWS - 1)
                return pl.ds(pl.multiple_of((row * blocks + wind.block(j)) * TILE, TILE), TILE)

            def code(u, j, spot=spot):
                return code_ref[spot(u, j), :]

            for m, cell_ref in enumerate(cell_refs):
                tiles = [[cell_ref[s, spot(u, j), :] for j in range(blocks)] for u in range(ROWS)]
                chains.append((wind, tiles, code, scalars.inflow(s, some[m])))
                places.append((s, slice(m * share, (m + 1) * share)))
        for c, (chain, state) in enumerate(zip(chains, substeps(chains))):
            keep(chain[0], state, packed.at[c])
        for c, place in enumerate(places):
            scatter(packed.at[c], scalars.me, [(out, place) for out in out_refs])
        return carry

    lax.fori_loop(0, total // together, sections, 0)


def outer_kernel(
    some, halos, starts, blocks, together, place_ref, ux_ref, uy_ref, inflow_ref, _,
    edge_ref, code_ref, *rest
):
    count = len(some)
    cell_refs, rest = rest[:count], rest[count:]
    halo_refs, rest = rest[: sum(halos)], rest[sum(halos) :]
    out_refs, (codes, packed) = rest[:-2], rest[-2:]
    total = cell_refs[0].shape[0]
    scalars = Scalars(place_ref, ux_ref, uy_ref, inflow_ref)
    me, odd = scalars.me, scalars.odd
    edge = SUB * blocks * TILE
    share = packed.shape[1] // len(out_refs)
    last = edge_ref.shape[0] - 2
    codes[:edge] = edge_ref[last + 1]
    codes[edge : 2 * edge] = edge_ref[last]
    codes[2 * edge :] = code_ref[...]

    def sections(turn, carry):
        chains, places = [], []
        for i in range(together):
            s = turn * together + i
            wind = scalars.wind(s, blocks)
            outside = jnp.where(wind.positive_x, 0, edge)
            second = jnp.logical_xor(wind.positive_x, odd == 1)

            def spot(u, j, wind=wind):
                if u < SUB:
                    row = wind.row(u, 0, SUB - 1)
                else:
                    row = wind.row(u, -SUB, ROWS + SUB - 1)
                return (row * blocks + wind.block(j)) * TILE

            def code(u, j, spot=spot, outside=outside):
                at = spot(u, j) + (outside if u < SUB else 2 * edge)
                return codes[pl.ds(pl.multiple_of(at, TILE), TILE), :]

            for m, cell_ref in enumerate(cell_refs):
                held = halo_refs[sum(halos[:m]) : sum(halos[: m + 1])]
                skip = starts[m] * edge
                tiles = []
                for u in range(ROWS):
                    row = []
                    for j in range(blocks):
                        at = spot(u, j) + (skip if u < SUB else 0)
                        at = pl.ds(pl.multiple_of(at, TILE), TILE)
                        if u >= SUB:
                            tile = cell_ref[s, at, :]
                        elif len(held) == 2:
                            tile = jnp.where(second, held[1][s, at, :], held[0][s, at, :])
                        else:
                            tile = held[0][s, at, :]
                        row.append(tile)
                    tiles.append(row)
                chains.append((wind, tiles, code, scalars.inflow(s, some[m])))
                places.append((s, slice(m * share, (m + 1) * share)))
        for c, (chain, state) in enumerate(zip(chains, substeps(chains))):
            keep(chain[0], state, packed.at[c])
        for c, place in enumerate(places):
            scatter(packed.at[c], me, [(out, place) for out in out_refs])
        return carry

    lax.fori_loop(0, total // together, sections, 0)
    if some[0] == 0:
        for s in range(total):
            line = jnp.full((1, LANES), scalars.ux(s), F32)
            for out in out_refs:
                out[total, s : s + 1, :] = line


def split_dot(weights, values):
    high = values.astype(BF16)
    rest = (values - high.astype(F32)).astype(BF16)
    return jnp.dot(
        weights, jnp.concatenate([high, rest, high], axis=0), preferred_element_type=F32
    )


def couple_kernel(first, base, groups, group_size, blocks, *refs):
    me_ref, rate_ref, share_ref, thermal_ref = refs[:4]
    refs = refs[4:]
    sign_refs, inner, outer = refs[:groups], refs[groups : 2 * groups], refs[2 * groups : 3 * groups]
    refs = refs[3 * groups :]
    if first:
        kernel_ref, spray_ref, gas_ref, merge_ref, *scratch = refs
    else:
        merge_ref, _, _, _, spray_ref, gas_ref, *scratch = refs
    rest, total = scratch
    spray_rows = spray_ref.reshape(spray_ref.shape[0] * spray_ref.shape[1], LANES)
    me = me_ref[0]
    moment, step = pl.program_id(0), pl.program_id(1)
    sections = groups * group_size
    size = ROWS * blocks
    half = size // 2
    steps = thermal_ref.shape[0] // size
    inner_spot = pl.ds(pl.multiple_of(((base + moment) * steps + step) * half, half), half)
    outer_spot = pl.ds(pl.multiple_of((moment * steps + step) * half, half), half)
    columns = pl.ds(pl.multiple_of(step * blocks * LANES, LANES), blocks * LANES)
    thermal = [
        thermal_ref[pl.ds(pl.multiple_of(step * size + i * half, half), half), :] for i in range(2)
    ]
    gas = tuple(jnp.zeros((half, LANES), F32) for _ in thermal)
    for k in range(groups):

        def section(s, sums, k=k):
            number = (me ^ k) * group_size + s
            flip = jnp.broadcast_to(sign_refs[k][group_size, pl.ds(s, 1), :], (half, LANES)) > 0.0
            rate = rate_ref[number]
            one, two = inner[k][s, inner_spot, :], outer[k][s, outer_spot, :]
            result = []
            for i, moved in enumerate((jnp.where(flip, two, one), jnp.where(flip, one, two))):
                evaporated = (rate * thermal[i]) * moved
                result.append(sums[i] + evaporated)
                rest[pl.ds(i * half * sections + number, half, stride=sections), :] = moved - evaporated
            return tuple(result)

        gas = lax.fori_loop(0, group_size, section, gas, unroll=4)
    for i in range(2):
        total[i * half : (i + 1) * half, :] = gas[i]
    for block in range(blocks):
        gas_ref[0, :, block * LANES : (block + 1) * LANES] = total[pl.ds(block, ROWS, stride=blocks), :]
    for row in range(ROWS):
        spots = [(row * blocks + block) * sections for block in range(blocks)]
        cells = jnp.concatenate([rest[spot : spot + sections, :] for spot in spots], axis=1)
        if first:
            merge = split_dot(kernel_ref[...], cells)
            merge_ref[row, :, columns] = merge
        else:
            merge = merge_ref[row, :, columns]
        flux = cells * merge
        result = cells - flux + split_dot(share_ref[...], flux)
        for block in range(blocks):
            spray_rows[pl.ds(block * ROWS + row, sections, stride=size), :] = result[
                :, block * LANES : (block + 1) * LANES
            ]


def params(limit=VMEM_LIMIT):
    return pltpu.CompilerParams(vmem_limit_bytes=limit)


def split_weights(weights):
    high = lax.reduce_precision(weights, 8, 7)
    return jnp.concatenate([high, high, weights - high], axis=1).astype(BF16)


def shards(
    droplet_integrals,
    flow_number_lengthwise,
    flow_number_crosswise,
    inflow_boundary_integrals,
    boundary_wall_indicator,
    inflow_indicator,
    collision_coefficient,
    collision_target_share,
    evaporation_speed_stepwise,
    thermal_factor,
):
    x, ux, uy = droplet_integrals, flow_number_lengthwise, flow_number_crosswise
    group_size, moments, rows, columns = x.shape
    groups = lax.axis_size("sec")
    slabs = lax.axis_size("space")
    sections = groups * group_size
    width = columns // groups
    blocks = columns // (TILE * LANES)
    size = columns // LANES * ROWS
    share_size = size // 2 // groups
    assert rows == ROWS and slabs % 2 == 0 and TILE % groups == 0

    swap = [(i, i ^ 1) for i in range(slabs)]
    outward = [(i, i + 2) for i in range(0, slabs - 2, 2)] + [(i, i - 2) for i in range(3, slabs, 2)]
    inward = [(j, i) for i, j in outward]

    smem = pl.BlockSpec(memory_space=pltpu.SMEM)
    anywhere = pl.BlockSpec(memory_space=pl.ANY)
    cells = stacked(x).reshape(group_size, moments * size, LANES)

    vmem = pl.BlockSpec(memory_space=pltpu.VMEM)
    edge = SUB * blocks * TILE
    place = jnp.stack([lax.axis_index("sec"), lax.axis_index("space") % 2]).astype(jnp.int32)

    def send(parts, first, last, *events):
        return [
            lax.ppermute(after(parts[k], *events), "sec", [(i, i ^ k) for i in range(groups)])
            for k in range(first, last)
        ]

    def after(value, *events):
        return lax.optimization_barrier((value, *events))[0]

    def select(outs):
        some = sum(outs, ())
        per_step = group_size // 2
        shapes = [
            (group_size + 2 * (i == 0), len(held) * edge, LANES) for i, held in enumerate(outs)
        ] + [(size, LANES)]
        kind = jnp.where(inflow_indicator > 0, 1.0, -1.0)
        kind = jnp.where(boundary_wall_indicator > 0, 0.0, kind).astype(F32)
        return pl.pallas_call(
            functools.partial(select_kernel, tuple(len(held) for held in outs), blocks),
            grid=(group_size // per_step,),
            in_specs=[smem]
            + [
                pl.BlockSpec((per_step, size, LANES), lambda g, moment=moment: (g, moment, 0))
                for moment in some
            ]
            + [vmem],
            out_specs=[vmem] * len(shapes),
            out_shape=[jax.ShapeDtypeStruct(shape, F32) for shape in shapes],
            compiler_params=params(SELECT_LIMIT),
            cost_estimate=cost(len(some), x.size),
            name="select_upwind_rows",
        )(after(ux, place), *[cells] * len(some), stacked(kind))

    def sort(outs, last):
        per_step = group_size // 4
        shapes = [(group_size, size, LANES)] * moments
        shapes += [(group_size, len(held) * edge, LANES) for held in outs]
        made = pl.pallas_call(
            functools.partial(sort_kernel, outs, blocks),
            grid=(group_size // per_step,),
            in_specs=[
                smem, pl.BlockSpec((per_step, moments * size, LANES), lambda g: (g, 0, 0))
            ],
            out_specs=[vmem] * len(shapes),
            out_shape=[jax.ShapeDtypeStruct(shape, F32) for shape in shapes],
            compiler_params=params(SORT_LIMIT),
            cost_estimate=cost(moments, x.size),
            name="sort_cells",
        )(after(ux, last), cells)
        return made[:moments], made[moments:]

    def cost(count, amount):
        return pl.CostEstimate(
            flops=amount * count, bytes_accessed=amount * count, transcendentals=0
        )

    def whole(kernel, name, last, operands, out_shapes, scratch=(), count=1):
        return pl.pallas_call(
            kernel,
            in_specs=[smem] * 4 + [anywhere] + [vmem] * len(operands),
            out_specs=[vmem] * len(out_shapes),
            out_shape=[jax.ShapeDtypeStruct(shape, F32) for shape in out_shapes],
            scratch_shapes=list(scratch),
            compiler_params=params(),
            cost_estimate=cost(count, x.size),
            name=name,
        )(place, ux, uy, inflow_boundary_integrals.T, last, *operands)

    def together(some):
        count = 1
        while 2 * count * len(some) <= CHAINS and group_size % (2 * count) == 0:
            count *= 2
        return count

    def transport_inner(some, last):
        return whole(
            functools.partial(inner_kernel, some, blocks, together(some)),
            "transport_inner_rows",
            last,
            [code, *[own[moment] for moment in some]],
            [(group_size, len(some) * share_size, LANES)] * groups,
            [pltpu.VMEM((together(some) * len(some), size // 2, LANES), F32)],
            count=len(some),
        )

    def transport_outer(some, halos, last, starts=None):
        return whole(
            functools.partial(
                outer_kernel,
                some,
                tuple(len(h) for h in halos),
                starts or (0,) * len(some),
                blocks,
                together(some),
            ),
            "transport_outer_rows",
            last,
            [near_0, code, *[own[moment] for moment in some], *sum(halos, ())],
            [(group_size + (some[0] == 0), len(some) * share_size, LANES)] * groups,
            [
                pltpu.VMEM((2 * edge + size, LANES), F32),
                pltpu.VMEM((together(some) * len(some), size // 2, LANES), F32),
            ],
            count=len(some),
        )

    def relay(own, far, count, last):
        return whole(
            functools.partial(relay_kernel, group_size),
            "relay_upwind_rows",
            last,
            [own, far],
            [(own.shape[0], own.shape[1] // count, LANES)] * count,
        )

    def swapped(array):
        return lax.ppermute(array, "space", swap)

    def hopped(array, pairs):
        return lax.ppermute(array, "space", pairs)

    share = split_weights(collision_target_share)
    kernel = split_weights(collision_coefficient)
    step_width = blocks * LANES
    steps = width // step_width
    step_size = ROWS * blocks
    thermal = thermal_factor.reshape(ROWS, steps, blocks, LANES).swapaxes(0, 1)
    thermal = thermal.reshape(steps * step_size, LANES)
    spray_type = jax.ShapeDtypeStruct((sections, moments * steps * step_size, LANES), F32)
    gas_type = jax.ShapeDtypeStruct((moments, rows, width), F32)
    merge_type = jax.ShapeDtypeStruct((rows, sections, width), F32)
    made = {}

    def couple(some, inner, base, outer, last):
        first = some[0] == 0

        in_specs = [smem] * 2 + [vmem] * (2 + 3 * groups)
        operands = [place, evaporation_speed_stepwise, share, after(thermal, last) if first else thermal]
        operands += list(made.setdefault("sign", outer)) + list(inner) + list(outer)
        out_specs = [
            pl.BlockSpec(
                (sections, step_size, LANES), lambda m, j: (0, (some[0] + m) * steps + j, 0)
            ),
            pl.BlockSpec((1, rows, step_width), lambda m, j: (some[0] + m, 0, j)),
        ]
        out_shape = [spray_type, gas_type]
        aliases = {}
        if first:
            in_specs.append(vmem)
            operands.append(kernel)
            out_specs.append(vmem)
            out_shape.append(merge_type)
        else:
            aliases = {len(operands) + 1: 0, len(operands) + 2: 1}
            in_specs += [vmem, anywhere, anywhere, anywhere]
            operands += [made["merge"], made["spray"], made["gas"], last]
        result = pl.pallas_call(
            functools.partial(couple_kernel, first, base, groups, group_size, blocks),
            grid=(len(some), steps),
            in_specs=in_specs,
            out_specs=out_specs,
            out_shape=out_shape,
            input_output_aliases=aliases,
            scratch_shapes=[
                pltpu.VMEM((sections * step_size, LANES), F32),
                pltpu.VMEM((step_size, LANES), F32),
            ],
            compiler_params=params(),
            cost_estimate=pl.CostEstimate(
                flops=sections * rows * width * sections * 2 * len(some),
                bytes_accessed=sections * rows * width * 12 * len(some),
                transcendentals=0,
            ),
            name="couple_sections",
        )(*operands)
        made.update(zip(("spray", "gas", "merge"), result))

    chosen_0, chosen_12, code = select(((0,), (1, 2)))
    near_12 = swapped(chosen_12)
    far_0 = hopped(chosen_0, inward)
    own, (chosen_34,) = sort(((3, 4),), code)
    far_34 = hopped(chosen_34, inward)
    inner = transport_inner(tuple(range(moments)), chosen_34)
    far_in = send(inner, 2, groups)
    (relayed_0,) = relay(chosen_0, far_0, 1, inner[0])
    near_0 = swapped(relayed_0)
    far_12 = hopped(after(near_12, relayed_0), outward)
    (relayed_34,) = relay(chosen_34, far_34, 1, after(relayed_0, near_0))
    near_34 = swapped(relayed_34)
    outer_0 = transport_outer((0,), ((near_0,),), after(relayed_34, far_in[-1]))
    far_of_0 = [part for k in range(2, groups) for part in send(outer_0, k, k + 1, far_in[k - 2])]
    pair_in = send(inner, 1, 2, outer_0[0], far_in[0])
    pair_of_0 = send(outer_0, 1, 2, *pair_in)
    outer_12 = transport_outer(
        (1, 2), ((near_12, far_12), (near_12, far_12)), after(outer_0[0], *far_of_0), (0, 1)
    )
    far_of_12 = send(outer_12, 2, 3) + send(outer_12, 3, groups, near_34)
    sent = [inner[0], *pair_in, *far_in]
    couple((0,), sent, 0, [outer_0[0], *pair_of_0, *far_of_0], outer_12[0])
    outer_3 = transport_outer((3,), ((near_34,),), after(made["merge"], far_of_12[0]), (0,))
    far_of_3 = send(outer_3, 2, groups)
    pair_of_12 = send(outer_12, 1, 2, near_34, *pair_of_0)
    outer_4 = transport_outer((4,), ((near_34,),), outer_3[0], (1,))
    pair_of_3 = send(outer_3, 1, 2, *pair_of_12)
    sent_4 = [outer_4[0]] + send(outer_4, 1, 2, *pair_of_3) + send(outer_4, 2, groups, *far_of_12)
    couple((1, 2), sent, 1, [outer_12[0], *pair_of_12, *far_of_12], outer_4[0])
    couple((3,), sent, 3, [outer_3[0], *pair_of_3, *far_of_3], outer_4[0])
    couple((4,), sent, 4, sent_4, outer_4[0])
    spray = jnp.swapaxes(
        made["spray"].reshape(sections, moments, width // LANES, rows, LANES), 2, 3
    )
    return spray.reshape(sections, moments, rows, width), made["gas"]


def solution(mesh):
    return jax.shard_map(
        shards,
        mesh=mesh,
        in_specs=(
            P("sec", None, "space", None),
            P("sec"),
            P("sec"),
            P("sec", None),
            P("space", None),
            P("space", None),
            P(),
            P(),
            P(),
            P("space", "sec"),
        ),
        out_specs=(P(None, None, "space", "sec"), P(None, "space", "sec")),
        check_vma=False,
    )
```

```python
import functools

import jax
import jax.numpy as jnp
from jax import lax
from jax.experimental import pallas as pl
from jax.experimental.pallas import tpu as pltpu
from jax.sharding import PartitionSpec as P

SUB = 4
ROWS = 2 * SUB
LANES = 128
TILE = 8
F32 = jnp.float32
BF16 = jnp.bfloat16
CHAINS = 10
SORT_LIMIT = 44 * 1024 * 1024
SELECT_LIMIT = 50 * 1024 * 1024
VMEM_LIMIT = 8 * 1024 * 1024


def stacked(array):
    *lead, rows, columns = array.shape
    tiles = columns // LANES
    array = array.reshape(*lead, rows, tiles, LANES)
    return jnp.swapaxes(array, -3, -2).reshape(*lead, rows * tiles, LANES)


class Scalars:
    def __init__(self, place_ref, ux_ref, uy_ref, inflow_ref):
        self.me, self.odd = place_ref[0], place_ref[1]
        self.ux_ref, self.uy_ref, self.inflow_ref = ux_ref, uy_ref, inflow_ref

    def ux(self, s):
        return self.ux_ref[s]

    def wind(self, s, blocks):
        return Wind(self.ux_ref[s], self.uy_ref[s], blocks)

    def inflow(self, s, moment):
        return self.inflow_ref[moment, s]


def sublane(shape=(TILE, LANES)):
    return lax.broadcasted_iota(jnp.int32, shape, 0)


class Wind:
    def __init__(self, speed_x, speed_y, blocks):
        self.a, self.b = jnp.abs(speed_x), jnp.abs(speed_y)
        self.own = 1.0 - self.a - self.b
        self.blocks = blocks
        self.positive_x = speed_x > 0.0
        self.positive_y = speed_y > 0.0
        lane = lax.broadcasted_iota(jnp.int32, (TILE, LANES), 1)
        self.lane_shift = jnp.where(self.positive_y, 1, LANES - 1).astype(jnp.int32)
        self.band_shift = jnp.where(self.positive_y, 1, TILE - 1).astype(jnp.int32)
        self.edge = lane == jnp.where(self.positive_y, 0, LANES - 1)
        self.border = sublane() == jnp.where(self.positive_y, 0, TILE - 1)

    def row(self, u, first, last):
        return jnp.where(self.positive_x, first + u, last - u)

    def block(self, j):
        return jnp.where(self.positive_y, j, self.blocks - 1 - j)


def substeps(chains):
    states = [chain[1] for chain in chains]
    for step in range(1, SUB + 1):
        fresh = []
        for (wind, _, code, value), state in zip(chains, states):
            rows = [None] * step
            for u in range(step, ROWS):
                turned = [pltpu.roll(tile, wind.lane_shift, axis=1) for tile in state[u]]
                wrap = pltpu.roll(turned[-1], wind.band_shift, axis=0)
                behind = [jnp.where(wind.border, 0.0, wrap)] + turned[:-1]
                tiles = []
                for j, tile in enumerate(state[u]):
                    side = jnp.where(wind.edge, behind[j], turned[j])
                    moved = wind.own * tile + wind.a * state[u - 1][j] + wind.b * side
                    kind = code(u, j)
                    tiles.append(jnp.where(kind < 0.0, moved, kind * value))
                rows.append(tiles)
            fresh.append(rows)
        states = fresh
    return states


def keep(wind, state, packed):
    blocks = wind.blocks
    for u in range(SUB, ROWS):
        row = wind.row(u, -SUB, ROWS - 1)
        for j, tile in enumerate(state[u]):
            packed[pl.ds(row * blocks + wind.block(j), TILE, stride=SUB * blocks), :] = tile


def scatter(packed, me, outs):
    share = packed.shape[0] // len(outs)
    for k, (out, spot) in enumerate(outs):
        start = pl.multiple_of((me ^ k) * share, share)
        out[spot] = packed[pl.ds(start, share), :]


def select_kernel(outs, blocks, ux_ref, *refs):
    count = sum(outs)
    x_refs, kind_ref, out_refs, code_ref = refs[:count], refs[count], refs[count + 1 : -1], refs[-1]
    per_step, size = x_refs[0].shape[:2]
    step = pl.program_id(0)
    edge = size // 2

    def section(s, carry):
        number = step * per_step + s
        first = jnp.where(ux_ref[number] > 0.0, SUB, 0)
        sources = iter(x_refs)
        for held, out_ref in zip(outs, out_refs):
            for i in range(held):
                x_ref = next(sources)
                for row in range(SUB):
                    for block in range(blocks):
                        spot = i * edge + (row * blocks + block) * TILE
                        source = pl.ds(block * ROWS + first + row, TILE, stride=blocks * ROWS)
                        out_ref[number, spot : spot + TILE, :] = x_ref[s, source, :]
        return carry

    lax.fori_loop(0, per_step, section, 0, unroll=2)

    @pl.when(step == 0)
    def _():
        last = out_refs[0].shape[0] - 2
        for row in range(ROWS):
            for block in range(blocks):
                spot = (row * blocks + block) * TILE
                source = pl.ds(block * ROWS + row, TILE, stride=blocks * ROWS)
                code_ref[spot : spot + TILE, :] = kind_ref[source, :]
        for i in range(2):
            out_refs[0][last + i] = code_ref[i * edge : (i + 1) * edge, :]


def sort_kernel(outs, blocks, ux_ref, x_ref, *refs):
    count = len(refs) - len(outs)
    cell_refs, out_refs = refs[:count], refs[count:]
    per_step = x_ref.shape[0]
    step = pl.program_id(0)
    size = cell_refs[0].shape[1]
    edge = size // 2

    def sort(source, target):
        for band in range(TILE):
            for block in range(blocks):
                tile = source((band * blocks + block) * ROWS)
                target[pl.ds(block * TILE + band, ROWS, stride=blocks * TILE), :] = tile

    def section(s, carry):
        number = step * per_step + s
        first = pl.multiple_of(jnp.where(ux_ref[number] > 0.0, edge, 0), edge)
        for m, cell_ref in enumerate(cell_refs):

            def source(spot, m=m):
                return x_ref[s, m * size + spot : m * size + spot + ROWS, :]

            sort(source, cell_ref.at[number])
        for held, out_ref in zip(outs, out_refs):
            for i, m in enumerate(held):
                out_ref[number, i * edge : (i + 1) * edge, :] = cell_refs[m][
                    number, pl.ds(first, edge), :
                ]
        return carry

    lax.fori_loop(0, per_step, section, 0)


def relay_kernel(total, place_ref, ux_ref, uy_ref, inflow_ref, _, own_ref, far_ref, *out_refs):
    scalars = Scalars(place_ref, ux_ref, uy_ref, inflow_ref)
    size = own_ref.shape[1] // len(out_refs)

    def relay(s, stays):
        def copy(source):
            for i, out_ref in enumerate(out_refs):
                out_ref[s] = source[s, i * size : (i + 1) * size, :]

        pl.when(stays)(lambda: copy(own_ref))
        pl.when(jnp.logical_not(stays))(lambda: copy(far_ref))

    def section(s, carry):
        relay(s, (scalars.ux(s) > 0.0) != (scalars.odd == 1))
        return carry

    lax.fori_loop(0, total, section, 0)
    if own_ref.shape[0] > total:
        relay(total, scalars.odd == 1)
        relay(total + 1, scalars.odd != 1)


def inner_kernel(
    some, blocks, together, place_ref, ux_ref, uy_ref, inflow_ref, _, code_ref, *rest
):
    count = len(some)
    cell_refs, out_refs, packed = rest[:count], rest[count:-1], rest[-1]
    total = cell_refs[0].shape[0]
    scalars = Scalars(place_ref, ux_ref, uy_ref, inflow_ref)
    share = packed.shape[1] // len(out_refs)

    def sections(turn, carry):
        chains, places = [], []
        for i in range(together):
            s = turn * together + i
            wind = scalars.wind(s, blocks)

            def spot(u, j, wind=wind):
                row = wind.row(u, 0, ROWS - 1)
                return pl.ds(pl.multiple_of((row * blocks + wind.block(j)) * TILE, TILE), TILE)

            def code(u, j, spot=spot):
                return code_ref[spot(u, j), :]

            for m, cell_ref in enumerate(cell_refs):
                tiles = [[cell_ref[s, spot(u, j), :] for j in range(blocks)] for u in range(ROWS)]
                chains.append((wind, tiles, code, scalars.inflow(s, some[m])))
                places.append((s, slice(m * share, (m + 1) * share)))
        for c, (chain, state) in enumerate(zip(chains, substeps(chains))):
            keep(chain[0], state, packed.at[c])
        for c, place in enumerate(places):
            scatter(packed.at[c], scalars.me, [(out, place) for out in out_refs])
        return carry

    lax.fori_loop(0, total // together, sections, 0)


def outer_kernel(
    some, halos, starts, blocks, together, place_ref, ux_ref, uy_ref, inflow_ref, _,
    edge_ref, code_ref, *rest
):
    count = len(some)
    cell_refs, rest = rest[:count], rest[count:]
    halo_refs, rest = rest[: sum(halos)], rest[sum(halos) :]
    out_refs, (codes, packed) = rest[:-2], rest[-2:]
    total = cell_refs[0].shape[0]
    scalars = Scalars(place_ref, ux_ref, uy_ref, inflow_ref)
    me, odd = scalars.me, scalars.odd
    edge = SUB * blocks * TILE
    share = packed.shape[1] // len(out_refs)
    last = edge_ref.shape[0] - 2
    codes[:edge] = edge_ref[last + 1]
    codes[edge : 2 * edge] = edge_ref[last]
    codes[2 * edge :] = code_ref[...]

    def sections(turn, carry):
        chains, places = [], []
        for i in range(together):
            s = turn * together + i
            wind = scalars.wind(s, blocks)
            outside = jnp.where(wind.positive_x, 0, edge)
            second = jnp.logical_xor(wind.positive_x, odd == 1)

            def spot(u, j, wind=wind):
                if u < SUB:
                    row = wind.row(u, 0, SUB - 1)
                else:
                    row = wind.row(u, -SUB, ROWS + SUB - 1)
                return (row * blocks + wind.block(j)) * TILE

            def code(u, j, spot=spot, outside=outside):
                at = spot(u, j) + (outside if u < SUB else 2 * edge)
                return codes[pl.ds(pl.multiple_of(at, TILE), TILE), :]

            for m, cell_ref in enumerate(cell_refs):
                held = halo_refs[sum(halos[:m]) : sum(halos[: m + 1])]
                skip = starts[m] * edge
                tiles = []
                for u in range(ROWS):
                    row = []
                    for j in range(blocks):
                        at = spot(u, j) + (skip if u < SUB else 0)
                        at = pl.ds(pl.multiple_of(at, TILE), TILE)
                        if u >= SUB:
                            tile = cell_ref[s, at, :]
                        elif len(held) == 2:
                            tile = jnp.where(second, held[1][s, at, :], held[0][s, at, :])
                        else:
                            tile = held[0][s, at, :]
                        row.append(tile)
                    tiles.append(row)
                chains.append((wind, tiles, code, scalars.inflow(s, some[m])))
                places.append((s, slice(m * share, (m + 1) * share)))
        for c, (chain, state) in enumerate(zip(chains, substeps(chains))):
            keep(chain[0], state, packed.at[c])
        for c, place in enumerate(places):
            scatter(packed.at[c], me, [(out, place) for out in out_refs])
        return carry

    lax.fori_loop(0, total // together, sections, 0)
    if some[0] == 0:
        for s in range(total):
            line = jnp.full((1, LANES), scalars.ux(s), F32)
            for out in out_refs:
                out[total, s : s + 1, :] = line


def split_dot(weights, values):
    high = values.astype(BF16)
    rest = (values - high.astype(F32)).astype(BF16)
    return jnp.dot(
        weights, jnp.concatenate([high, rest, high], axis=0), preferred_element_type=F32
    )


def couple_kernel(first, base, groups, group_size, blocks, *refs):
    me_ref, rate_ref, share_ref, thermal_ref = refs[:4]
    refs = refs[4:]
    sign_refs, inner, outer = refs[:groups], refs[groups : 2 * groups], refs[2 * groups : 3 * groups]
    refs = refs[3 * groups :]
    if first:
        kernel_ref, spray_ref, gas_ref, merge_ref, *scratch = refs
    else:
        merge_ref, _, _, _, spray_ref, gas_ref, *scratch = refs
    rest, total = scratch
    spray_rows = spray_ref.reshape(spray_ref.shape[0] * spray_ref.shape[1], LANES)
    me = me_ref[0]
    moment, step = pl.program_id(0), pl.program_id(1)
    sections = groups * group_size
    size = ROWS * blocks
    half = size // 2
    steps = thermal_ref.shape[0] // size
    inner_spot = pl.ds(pl.multiple_of(((base + moment) * steps + step) * half, half), half)
    outer_spot = pl.ds(pl.multiple_of((moment * steps + step) * half, half), half)
    columns = pl.ds(pl.multiple_of(step * blocks * LANES, LANES), blocks * LANES)
    thermal = [
        thermal_ref[pl.ds(pl.multiple_of(step * size + i * half, half), half), :] for i in range(2)
    ]
    gas = tuple(jnp.zeros((half, LANES), F32) for _ in thermal)
    for k in range(groups):

        def section(s, sums, k=k):
            number = (me ^ k) * group_size + s
            flip = jnp.broadcast_to(sign_refs[k][group_size, pl.ds(s, 1), :], (half, LANES)) > 0.0
            rate = rate_ref[number]
            one, two = inner[k][s, inner_spot, :], outer[k][s, outer_spot, :]
            result = []
            for i, moved in enumerate((jnp.where(flip, two, one), jnp.where(flip, one, two))):
                evaporated = (rate * thermal[i]) * moved
                result.append(sums[i] + evaporated)
                rest[pl.ds(i * half * sections + number, half, stride=sections), :] = moved - evaporated
            return tuple(result)

        gas = lax.fori_loop(0, group_size, section, gas, unroll=16)
    for i in range(2):
        total[i * half : (i + 1) * half, :] = gas[i]
    for block in range(blocks):
        gas_ref[0, :, block * LANES : (block + 1) * LANES] = total[pl.ds(block, ROWS, stride=blocks), :]
    for row in range(ROWS):
        spots = [(row * blocks + block) * sections for block in range(blocks)]
        cells = jnp.concatenate([rest[spot : spot + sections, :] for spot in spots], axis=1)
        if first:
            merge = split_dot(kernel_ref[...], cells)
            merge_ref[row, :, columns] = merge
        else:
            merge = merge_ref[row, :, columns]
        flux = cells * merge
        result = cells - flux + split_dot(share_ref[...], flux)
        for block in range(blocks):
            spray_rows[pl.ds(block * ROWS + row, sections, stride=size), :] = result[
                :, block * LANES : (block + 1) * LANES
            ]


def params(limit=VMEM_LIMIT):
    return pltpu.CompilerParams(vmem_limit_bytes=limit)


def split_weights(weights):
    high = lax.reduce_precision(weights, 8, 7)
    return jnp.concatenate([high, high, weights - high], axis=1).astype(BF16)


def shards(
    droplet_integrals,
    flow_number_lengthwise,
    flow_number_crosswise,
    inflow_boundary_integrals,
    boundary_wall_indicator,
    inflow_indicator,
    collision_coefficient,
    collision_target_share,
    evaporation_speed_stepwise,
    thermal_factor,
):
    x, ux, uy = droplet_integrals, flow_number_lengthwise, flow_number_crosswise
    group_size, moments, rows, columns = x.shape
    groups = lax.axis_size("sec")
    slabs = lax.axis_size("space")
    sections = groups * group_size
    width = columns // groups
    blocks = columns // (TILE * LANES)
    size = columns // LANES * ROWS
    share_size = size // 2 // groups
    assert rows == ROWS and slabs % 2 == 0 and TILE % groups == 0

    swap = [(i, i ^ 1) for i in range(slabs)]
    outward = [(i, i + 2) for i in range(0, slabs - 2, 2)] + [(i, i - 2) for i in range(3, slabs, 2)]
    inward = [(j, i) for i, j in outward]

    smem = pl.BlockSpec(memory_space=pltpu.SMEM)
    anywhere = pl.BlockSpec(memory_space=pl.ANY)
    cells = stacked(x).reshape(group_size, moments * size, LANES)

    vmem = pl.BlockSpec(memory_space=pltpu.VMEM)
    edge = SUB * blocks * TILE
    place = jnp.stack([lax.axis_index("sec"), lax.axis_index("space") % 2]).astype(jnp.int32)

    def send(parts, first, last, *events):
        return [
            lax.ppermute(after(parts[k], *events), "sec", [(i, i ^ k) for i in range(groups)])
            for k in range(first, last)
        ]

    def after(value, *events):
        return lax.optimization_barrier((value, *events))[0]

    def select(outs):
        some = sum(outs, ())
        per_step = group_size // 2
        shapes = [
            (group_size + 2 * (i == 0), len(held) * edge, LANES) for i, held in enumerate(outs)
        ] + [(size, LANES)]
        kind = jnp.where(inflow_indicator > 0, 1.0, -1.0)
        kind = jnp.where(boundary_wall_indicator > 0, 0.0, kind).astype(F32)
        return pl.pallas_call(
            functools.partial(select_kernel, tuple(len(held) for held in outs), blocks),
            grid=(group_size // per_step,),
            in_specs=[smem]
            + [
                pl.BlockSpec((per_step, size, LANES), lambda g, moment=moment: (g, moment, 0))
                for moment in some
            ]
            + [vmem],
            out_specs=[vmem] * len(shapes),
            out_shape=[jax.ShapeDtypeStruct(shape, F32) for shape in shapes],
            compiler_params=params(SELECT_LIMIT),
            cost_estimate=cost(len(some), x.size),
            name="select_upwind_rows",
        )(after(ux, place), *[cells] * len(some), stacked(kind))

    def sort(outs, last):
        per_step = group_size // 4
        shapes = [(group_size, size, LANES)] * moments
        shapes += [(group_size, len(held) * edge, LANES) for held in outs]
        made = pl.pallas_call(
            functools.partial(sort_kernel, outs, blocks),
            grid=(group_size // per_step,),
            in_specs=[
                smem, pl.BlockSpec((per_step, moments * size, LANES), lambda g: (g, 0, 0))
            ],
            out_specs=[vmem] * len(shapes),
            out_shape=[jax.ShapeDtypeStruct(shape, F32) for shape in shapes],
            compiler_params=params(SORT_LIMIT),
            cost_estimate=cost(moments, x.size),
            name="sort_cells",
        )(after(ux, last), cells)
        return made[:moments], made[moments:]

    def cost(count, amount):
        return pl.CostEstimate(
            flops=amount * count, bytes_accessed=amount * count, transcendentals=0
        )

    def whole(kernel, name, last, operands, out_shapes, scratch=(), count=1):
        return pl.pallas_call(
            kernel,
            in_specs=[smem] * 4 + [anywhere] + [vmem] * len(operands),
            out_specs=[vmem] * len(out_shapes),
            out_shape=[jax.ShapeDtypeStruct(shape, F32) for shape in out_shapes],
            scratch_shapes=list(scratch),
            compiler_params=params(),
            cost_estimate=cost(count, x.size),
            name=name,
        )(place, ux, uy, inflow_boundary_integrals.T, last, *operands)

    def together(some):
        count = 1
        while 2 * count * len(some) <= CHAINS and group_size % (2 * count) == 0:
            count *= 2
        return count

    def transport_inner(some, last):
        return whole(
            functools.partial(inner_kernel, some, blocks, together(some)),
            "transport_inner_rows",
            last,
            [code, *[own[moment] for moment in some]],
            [(group_size, len(some) * share_size, LANES)] * groups,
            [pltpu.VMEM((together(some) * len(some), size // 2, LANES), F32)],
            count=len(some),
        )

    def transport_outer(some, halos, last, starts=None):
        return whole(
            functools.partial(
                outer_kernel,
                some,
                tuple(len(h) for h in halos),
                starts or (0,) * len(some),
                blocks,
                together(some),
            ),
            "transport_outer_rows",
            last,
            [near_0, code, *[own[moment] for moment in some], *sum(halos, ())],
            [(group_size + (some[0] == 0), len(some) * share_size, LANES)] * groups,
            [
                pltpu.VMEM((2 * edge + size, LANES), F32),
                pltpu.VMEM((together(some) * len(some), size // 2, LANES), F32),
            ],
            count=len(some),
        )

    def relay(own, far, count, last):
        return whole(
            functools.partial(relay_kernel, group_size),
            "relay_upwind_rows",
            last,
            [own, far],
            [(own.shape[0], own.shape[1] // count, LANES)] * count,
        )

    def swapped(array):
        return lax.ppermute(array, "space", swap)

    def hopped(array, pairs):
        return lax.ppermute(array, "space", pairs)

    share = split_weights(collision_target_share)
    kernel = split_weights(collision_coefficient)
    step_width = blocks * LANES
    steps = width // step_width
    step_size = ROWS * blocks
    thermal = thermal_factor.reshape(ROWS, steps, blocks, LANES).swapaxes(0, 1)
    thermal = thermal.reshape(steps * step_size, LANES)
    spray_type = jax.ShapeDtypeStruct((sections, moments * steps * step_size, LANES), F32)
    gas_type = jax.ShapeDtypeStruct((moments, rows, width), F32)
    merge_type = jax.ShapeDtypeStruct((rows, sections, width), F32)
    made = {}

    def couple(some, inner, base, outer, last):
        first = some[0] == 0

        in_specs = [smem] * 2 + [vmem] * (2 + 3 * groups)
        operands = [place, evaporation_speed_stepwise, share, after(thermal, last) if first else thermal]
        operands += list(made.setdefault("sign", outer)) + list(inner) + list(outer)
        out_specs = [
            pl.BlockSpec(
                (sections, step_size, LANES), lambda m, j: (0, (some[0] + m) * steps + j, 0)
            ),
            pl.BlockSpec((1, rows, step_width), lambda m, j: (some[0] + m, 0, j)),
        ]
        out_shape = [spray_type, gas_type]
        aliases = {}
        if first:
            in_specs.append(vmem)
            operands.append(kernel)
            out_specs.append(vmem)
            out_shape.append(merge_type)
        else:
            aliases = {len(operands) + 1: 0, len(operands) + 2: 1}
            in_specs += [vmem, anywhere, anywhere, anywhere]
            operands += [made["merge"], made["spray"], made["gas"], last]
        result = pl.pallas_call(
            functools.partial(couple_kernel, first, base, groups, group_size, blocks),
            grid=(len(some), steps),
            in_specs=in_specs,
            out_specs=out_specs,
            out_shape=out_shape,
            input_output_aliases=aliases,
            scratch_shapes=[
                pltpu.VMEM((sections * step_size, LANES), F32),
                pltpu.VMEM((step_size, LANES), F32),
            ],
            compiler_params=params(),
            cost_estimate=pl.CostEstimate(
                flops=sections * rows * width * sections * 2 * len(some),
                bytes_accessed=sections * rows * width * 12 * len(some),
                transcendentals=0,
            ),
            name="couple_sections",
        )(*operands)
        made.update(zip(("spray", "gas", "merge"), result))

    chosen_0, chosen_12, code = select(((0,), (1, 2)))
    near_12 = swapped(chosen_12)
    far_0 = hopped(chosen_0, inward)
    own, (chosen_34,) = sort(((3, 4),), code)
    far_34 = hopped(chosen_34, inward)
    inner = transport_inner(tuple(range(moments)), chosen_34)
    far_in = send(inner, 2, groups)
    (relayed_0,) = relay(chosen_0, far_0, 1, inner[0])
    near_0 = swapped(relayed_0)
    far_12 = hopped(after(near_12, relayed_0), outward)
    (relayed_34,) = relay(chosen_34, far_34, 1, after(relayed_0, near_0))
    near_34 = swapped(relayed_34)
    outer_0 = transport_outer((0,), ((near_0,),), after(relayed_34, far_in[-1]))
    far_of_0 = [part for k in range(2, groups) for part in send(outer_0, k, k + 1, far_in[k - 2])]
    pair_in = send(inner, 1, 2, outer_0[0], far_in[0])
    pair_of_0 = send(outer_0, 1, 2, *pair_in)
    outer_12 = transport_outer(
        (1, 2), ((near_12, far_12), (near_12, far_12)), after(outer_0[0], *far_of_0), (0, 1)
    )
    far_of_12 = send(outer_12, 2, 3) + send(outer_12, 3, groups, near_34)
    sent = [inner[0], *pair_in, *far_in]
    couple((0,), sent, 0, [outer_0[0], *pair_of_0, *far_of_0], outer_12[0])
    outer_3 = transport_outer((3,), ((near_34,),), after(made["merge"], far_of_12[0]), (0,))
    far_of_3 = send(outer_3, 2, groups)
    pair_of_12 = send(outer_12, 1, 2, near_34, *pair_of_0)
    outer_4 = transport_outer((4,), ((near_34,),), outer_3[0], (1,))
    pair_of_3 = send(outer_3, 1, 2, *pair_of_12)
    sent_4 = [outer_4[0]] + send(outer_4, 1, 2, *pair_of_3) + send(outer_4, 2, groups, *far_of_12)
    couple((1, 2), sent, 1, [outer_12[0], *pair_of_12, *far_of_12], outer_4[0])
    couple((3,), sent, 3, [outer_3[0], *pair_of_3, *far_of_3], outer_4[0])
    couple((4,), sent, 4, sent_4, outer_4[0])
    spray = jnp.swapaxes(
        made["spray"].reshape(sections, moments, width // LANES, rows, LANES), 2, 3
    )
    return spray.reshape(sections, moments, rows, width), made["gas"]


def solution(mesh):
    return jax.shard_map(
        shards,
        mesh=mesh,
        in_specs=(
            P("sec", None, "space", None),
            P("sec"),
            P("sec"),
            P("sec", None),
            P("space", None),
            P("space", None),
            P(),
            P(),
            P(),
            P("space", "sec"),
        ),
        out_specs=(P(None, None, "space", "sec"), P(None, "space", "sec")),
        check_vma=False,
    )
```
